512 devices in a mesh: patch: 4 (over x), curve: 128 (over z, y, core).
Axes of the slice: x: 4, y: 8, z: 8, core: 2. Of those that a mesh axis runs over, the one named last changes fastest.
Arguments:
- points: bfloat16 [128, 4, 256, 512], P('curve', 'patch'), may hold values from -6 to 6
- norm_gain_one: float32 [512], replicated, may hold values from 0.4 to 2.5, as said below
- qkv_one: bfloat16 [512, 1536], replicated, may hold values from -0.25 to 0.25
- out_one: bfloat16 [512, 512], replicated, may hold values from -0.25 to 0.25
- hilbert_pos: int32 [128, 4, 256], P('curve', 'patch'), may hold values from 0 to 32767, as said below
- norm_gain_two: float32 [512], replicated, may hold values from 0.4 to 2.5, as said below
- qkv_two: bfloat16 [512, 1536], replicated, may hold values from -0.25 to 0.25
- out_two: bfloat16 [512, 512], replicated, may hold values from -0.25 to 0.25
- hilbert_seg: int32 [4, 128, 256], P('patch', 'curve'), may hold values from 0 to 7, never falling along the last dimension, each value on 1 to 128 neighbouring positions
- out_grad: bfloat16 [4, 128, 256, 512], P('patch', 'curve'), may hold values from -6 to 6
Outputs:
- point_grad: bfloat16 [128, 4, 256, 512], P('curve', 'patch')
The draws below stay inside these ranges and needn't reach their ends.
Inputs may be any that keep to these rules, and one draw needn't show every extreme that they name: `hilbert_pos`: for each index p of the second dimension, the values over all c and i form a permutation of 0 to 32767. From the points of one device at most 4 have q // 256 equal to any one value, and in every draw some device sends exactly 4 to some owner. `hilbert_seg`: within one device's slots the numbers never fall; a patch holds at most 128 slots. `norm_gain_one`: positive gains. `norm_gain_two`: positive gains.
All inputs are finite; a program needn't handle non-finite values.
Results may differ from the reference program's by a relative error of at most 0.02.
Values may be sent and summed in bfloat16 or wider, within the bound.
A program may use at most 64 MiB of HBM per device.

```python
import math
import jax
import jax.numpy as jnp
import numpy as np
from jax import lax

D = 512
HEADS = 16
ROWS = 256
SEG_COUNT = 8
SEG_MOST = 128
PATCH = 1024
N_PATCH = 4
N_CURVE = 128


def pair_counts(key):
    base = ROWS // N_CURVE
    half = N_CURVE // 2
    extra = jax.random.randint(jax.random.fold_in(key, 1), (half,), 0, base + 1)
    extra = extra.at[0].set(base)
    counts = jnp.concatenate([base + extra, base - extra])
    counts = counts[jax.random.permutation(jax.random.fold_in(key, 2), N_CURVE)]
    labels = jax.random.permutation(jax.random.fold_in(key, 3), N_CURVE)
    return counts[(labels[None, :] - labels[:, None]) % N_CURVE]


def group_positions(key):
    pairs = pair_counts(key)
    slots = jnp.arange(ROWS)

    def one_source(counts_row, source_key):
        ends = jnp.cumsum(counts_row)
        starts = ends - counts_row
        owner = jnp.repeat(jnp.arange(N_CURVE), counts_row, total_repeat_length=ROWS)
        ranking = slots - starts[owner]
        shuffle = jax.random.permutation(source_key, ROWS)
        return (owner[shuffle], ranking[shuffle])
    source_keys = jax.random.split(jax.random.fold_in(key, 4), N_CURVE)
    owner, ranking = jax.vmap(one_source)(pairs, source_keys)
    incoming_base = jnp.cumsum(pairs, axis=0) - pairs
    incoming = incoming_base[jnp.arange(N_CURVE)[:, None], owner] + ranking
    dest_keys = jax.random.split(jax.random.fold_in(key, 5), N_CURVE)
    shuffles = jax.vmap(lambda dest_key: jax.random.permutation(dest_key, ROWS))(dest_keys)
    offset = shuffles[owner, incoming]
    return owner * ROWS + offset


def draw_hilbert_pos(key, part):
    groups = [group_positions(jax.random.fold_in(key, 100 + index)) for index in range(N_PATCH)]
    return jnp.stack(groups, axis=1).astype(jnp.int32)


def gain_values(key):
    return jnp.exp(jax.random.uniform(key, (D,), jnp.float32, math.log(0.5), math.log(2.0)))


def draw_norm_gain_one(key, part):
    return gain_values(jax.random.fold_in(key, 7))


def draw_norm_gain_two(key, part):
    return gain_values(jax.random.fold_in(key, 8))


def shard_levels(rng, extent, cuts, smallest, top_value):
    factor_of = 1.0
    for position, blocks in cuts:
        draws = jax.random.uniform(jax.random.fold_in(jax.random.fold_in(rng, 6), position), (blocks,), jnp.float32, smallest / len(cuts), top_value / len(cuts))
        factor_of = factor_of * jnp.repeat(jnp.exp(draws), extent[position] // blocks).reshape((-1,) + (1,) * (len(extent) - 1 - position))
    return factor_of


def split_up(number_of, total, limit, skew):
    loads = [(1 << 20) // math.isqrt(grade ** skew) + 1 for grade in range(2, number_of + 1)]
    spare, given = total - limit - (number_of - 1), [1] * (number_of - 1)
    while spare > 0:
        movable = [i for i in range(number_of - 1) if given[i] < limit]
        mass, left = sum([loads[i] for i in movable]), spare
        for i in movable:
            addition = min(limit - given[i], max(1, left * loads[i] // mass), spare)
            given[i] = given[i] + addition
            spare = spare - addition
    return np.array([limit] + given)


def uneven(own_key, count, total, reach, slope):
    if count == 2:
        one = jax.random.randint(own_key, (), max(1, total - reach), min(reach, total - 1) + 1)
        return jnp.stack([one, total - one])
    lengths = jnp.asarray(split_up(count, total, reach, slope), jnp.int32)
    twos = (count - 1) // 2
    source_of, sink = lengths[1:1 + 2 * twos:2], lengths[2:2 + 2 * twos:2]
    room = jnp.minimum(source_of - 1, reach - sink)
    passed = jax.random.randint(jax.random.fold_in(own_key, 1), (twos,), 0, 1 << 20) % (room + 1)
    lengths = lengths.at[1:1 + 2 * twos:2].set(source_of - passed).at[2:2 + 2 * twos:2].set(sink + passed)
    return lengths[jax.random.permutation(jax.random.fold_in(own_key, 2), count)]


def bell_draw(own_key, extent, deviation, bound, cuts=(), dtype=jnp.bfloat16):
    drawn = jax.random.normal(own_key, extent, jnp.float32) * deviation
    if len(cuts) > 0:
        drawn = shard_levels(own_key, extent, cuts, -0.22, 0.18) * drawn
    return jnp.clip(drawn, min=-bound, max=bound).astype(dtype)


def setup_inputs(seed: int = 0) -> dict:
    seeds = jax.random.split(jax.random.key(seed), 11)
    points = bell_draw(seeds[0], (N_CURVE, N_PATCH, ROWS, D), 1.0, 6.0, ((0, 128), (1, 4)))
    norm_gain_one = draw_norm_gain_one(jax.random.fold_in(seeds[10], 71), 0)
    qkv_one = bell_draw(seeds[2], (D, 3 * D), D ** -0.5, 0.25)
    out_one = bell_draw(seeds[3], (D, D), D ** -0.5, 0.25)
    hilbert_pos = draw_hilbert_pos(jax.random.fold_in(seeds[10], 71), 0)
    norm_gain_two = draw_norm_gain_two(jax.random.fold_in(seeds[10], 71), 0)
    qkv_two = bell_draw(seeds[6], (D, 3 * D), D ** -0.5, 0.25)
    out_two = bell_draw(seeds[7], (D, D), D ** -0.5, 0.25)
    hilbert_seg = jax.vmap(lambda own: jnp.searchsorted(jnp.cumsum(uneven(own, SEG_COUNT, ROWS, SEG_MOST, 2)), jnp.arange(ROWS), side="right"))(jax.random.split(seeds[8], N_PATCH * N_CURVE)).reshape((N_PATCH, N_CURVE, ROWS)).astype(jnp.int32)
    out_grad = bell_draw(seeds[9], (N_PATCH, N_CURVE, ROWS, D), 1.0, 6.0, ((0, 4), (1, 128)))
    return dict(points=points, norm_gain_one=norm_gain_one, qkv_one=qkv_one, out_one=out_one, hilbert_pos=hilbert_pos, norm_gain_two=norm_gain_two, qkv_two=qkv_two, out_two=out_two, hilbert_seg=hilbert_seg, out_grad=out_grad)


EPS = 1e-06

def prepare(source_rows, gain, w_qkv):
    wide = source_rows.astype(jnp.float32)
    power = lax.optimization_barrier(jnp.mean(wide * wide, axis=-1, keepdims=True))
    normed = (wide * lax.rsqrt(power + EPS) * gain).astype(jnp.bfloat16)
    return jnp.dot(normed, w_qkv, preferred_element_type=jnp.float32).astype(jnp.bfloat16)

def finish(source_rows, mixed, w_out):
    total = source_rows.astype(jnp.float32) + jnp.dot(mixed, w_out, preferred_element_type=jnp.float32)
    return total.astype(jnp.bfloat16)

def attend(queries, keys, values, allowed):
    count, width = queries.shape
    depth = width // HEADS
    q_heads = queries.astype(jnp.float32).reshape(count, HEADS, depth)
    k_heads = keys.astype(jnp.float32).reshape(-1, HEADS, depth)
    v_heads = values.astype(jnp.float32).reshape(-1, HEADS, depth)
    scores = jnp.einsum('rhe,khe->hrk', q_heads, k_heads) * depth ** (-0.5)
    if allowed is not None:
        scores = jnp.where(allowed[None], scores, -1e+30)
    weights = jax.nn.softmax(scores, axis=-1)
    rounded = lax.optimization_barrier(weights.astype(jnp.bfloat16))
    mixed = jnp.einsum('hrk,khe->rhe', rounded.astype(jnp.float32), v_heads)
    return mixed.reshape(count, width).astype(jnp.bfloat16)

def device_block(source_rows, segment, gain, w_qkv, w_out):
    width = source_rows.shape[1]
    packed = prepare(source_rows, gain, w_qkv)
    allowed = segment[:, None] == segment[None, :]
    mixed = attend(packed[:, :width], packed[:, width:2 * width], packed[:, 2 * width:], allowed)
    return finish(source_rows, mixed, w_out)

def reference(points, norm_gain_one, qkv_one, out_one, hilbert_pos, norm_gain_two, qkv_two, out_two, hilbert_seg, out_grad):
    width = points.shape[-1]

    def patch_block(patch_rows):
        packed = prepare(patch_rows, norm_gain_one, qkv_one)
        mixed = attend(packed[:, :width], packed[:, width:2 * width], packed[:, 2 * width:], None)
        return finish(patch_rows, mixed, out_one)

    def second_block(pair):
        return device_block(pair[0], pair[1], norm_gain_two, qkv_two, out_two)

    def forward(source):
        patches = source.reshape(N_CURVE, PATCH, width)
        moved = lax.map(jax.checkpoint(patch_block), patches)
        grouped = moved.reshape(N_CURVE, N_PATCH, ROWS, width).transpose(1, 0, 2, 3).reshape(N_PATCH, N_CURVE * ROWS, width)
        order = hilbert_pos.transpose(1, 0, 2).reshape(N_PATCH, N_CURVE * ROWS)
        placed = jax.vmap(lambda src, where_to: jnp.zeros_like(src).at[where_to].set(src))(grouped, order)
        blocks = placed.reshape(N_PATCH * N_CURVE, ROWS, width)
        segments = hilbert_seg.reshape(N_PATCH * N_CURVE, ROWS)
        done = lax.map(jax.checkpoint(second_block), (blocks, segments))
        return done.reshape(N_PATCH, N_CURVE, ROWS, width)
    _, pull = jax.vjp(forward, points)
    return pull(out_grad)[0]
```

```python
import functools
import math

import jax
import jax.numpy as jnp
from jax import lax
from jax.experimental import pallas as pl
from jax.experimental.pallas import tpu as pltpu
from jax.sharding import PartitionSpec as P

HEADS = 16
EPS = 1e-06
F32 = jnp.float32
BF = jnp.bfloat16
MESH = pl.DeviceIdType.MESH
LANES = 128


def dot(a, b):
    return lax.dot_general(a, b, (((1,), (0,)), ((), ())), preferred_element_type=F32)


def dot_nt(a, b):
    return lax.dot_general(a, b, (((1,), (1,)), ((), ())), preferred_element_type=F32)


def dot_tn(a, b):
    return lax.dot_general(a, b, (((0,), (0,)), ((), ())), preferred_element_type=F32)


def iota(shape, dim):
    return lax.broadcasted_iota(jnp.int32, shape, dim)


def norm_scale(rows):
    return lax.rsqrt(jnp.mean(rows * rows, axis=-1, keepdims=True) + EPS)


def norm_grad(rows, gain, cot):
    r = norm_scale(rows)
    c = cot * gain
    inner = jnp.mean(c * rows, axis=-1, keepdims=True)
    return r * (c - rows * (r * r * inner))


def column(row, size):
    eye = iota((size, size), 0) == iota((size, size), 1)
    return jnp.sum(jnp.where(eye, row, 0.0), axis=1, keepdims=True)


def kernel(
    NP, NC, R, D, CAP, DEPTH,
    x_hbm, w1_hbm, o1_hbm, w2_hbm, o2_hbm, og_hbm, gain1, gain2, pos, seg,
    out,
    x, w1, o1, w2, o2, og,
    qkv_s, qkv_r, va, ex, inv_all, mix_all,
    mix_s, mix_r, at_s, at_r, tmp, a_s, a_r, b_s, b_r,
    pk, gat, p2, p2t, bias, hil, two, gtwo, dtwo,
    g_s, g_r, dq_acc, d_s, d_r,
    lsem, xs_sem, xr_sem, ms_sem, mr_sem, cs_sem, cr_sem, gs_sem, gr_sem, ds_sem, dr_sem,
):
    me_p = lax.axis_index("patch")
    me_c = lax.axis_index("curve")
    scale = DEPTH ** (-0.5)
    to_log2 = scale * math.log2(math.e)
    from_log2 = math.log(2.0)
    per = LANES // DEPTH
    KEYS = NP * R
    SLOTS = CAP * NC

    loads = [
        pltpu.make_async_copy(src, dst, lsem.at[i])
        for i, (src, dst) in enumerate(
            [(x_hbm, x), (w1_hbm, w1), (o1_hbm, o1), (w2_hbm, w2), (o2_hbm, o2), (og_hbm, og)]
        )
    ]
    for load in loads:
        load.start()

    barrier = pltpu.get_barrier_semaphore()

    def peer(k):
        return lax.rem(me_p + k, NP)

    for k in range(1, NP):
        pl.semaphore_signal(barrier, inc=1, device_id=(peer(k), me_c), device_id_type=MESH)

    @pl.loop(1, NC)
    def _(k):
        pl.semaphore_signal(
            barrier, inc=1, device_id=(me_p, lax.rem(me_c + k, NC)), device_id_type=MESH
        )

    def head_mask(rows, h):
        return iota((rows, LANES), 1) // DEPTH == h

    loads[0].wait()
    loads[1].wait()
    rows = x[...].astype(F32)
    normed = (rows * norm_scale(rows) * gain1[...]).astype(BF)
    for j in (1, 2, 0):
        part = dot(normed, w1[:, j * D : (j + 1) * D])
        part = (part * to_log2 if j == 0 else part).astype(BF)
        for p in range(NP):
            qkv_s[j, p] = part[:, p * LANES : (p + 1) * LANES]

    pl.semaphore_wait(barrier, NP - 1 + NC - 1)

    my_rows = pl.ds(pl.multiple_of(me_p * R, R), R)
    for j in (1, 2, 0):
        for k in range(1, NP):
            pltpu.make_async_remote_copy(
                src_ref=qkv_s.at[j, peer(k)],
                dst_ref=qkv_r.at[j, my_rows],
                send_sem=xs_sem,
                recv_sem=xr_sem.at[j],
                device_id=(peer(k), me_c),
                device_id_type=MESH,
            ).start()
        qkv_r[j, my_rows, :] = qkv_s[j, me_p]

    place = pos[...]
    owner_row = (place // R).astype(F32)
    offset_row = (place % R).astype(F32)
    owner_col = column(owner_row, R)
    offset_col = column(offset_row, R)
    same = owner_col == owner_row
    i0, i1 = iota((R, R), 0), iota((R, R), 1)
    rank_row = jnp.sum(jnp.where(same & (i0 < i1), 1.0, 0.0), axis=0, keepdims=True)
    rank_col = jnp.sum(jnp.where(same & (i1 < i0), 1.0, 0.0), axis=1, keepdims=True)
    slot_row = rank_row * NC + owner_row
    slot_col = rank_col * NC + owner_col
    pk[...] = jnp.where(iota((SLOTS, R), 0).astype(F32) == slot_row, 1.0, 0.0).astype(BF)
    gat[...] = jnp.where(iota((R, SLOTS), 1).astype(F32) == slot_col, 1.0, 0.0).astype(BF)
    table = dot(pk[...], jnp.broadcast_to(offset_col + 1.0, (R, LANES)).astype(BF))
    lane = iota((NC, LANES), 1)
    note = jnp.zeros((NC, LANES), F32)
    for r in range(CAP):
        note = jnp.where(lane == r, table[r * NC : (r + 1) * NC], note)
    at_s[...] = note.reshape(NC, 1, LANES)

    def spread(src, dst, send_sem, recv_sem):
        @pl.loop(1, NC)
        def _(k):
            other = lax.rem(me_c + k, NC)
            pltpu.make_async_remote_copy(
                src_ref=src.at[other],
                dst_ref=dst.at[me_c],
                send_sem=send_sem,
                recv_sem=recv_sem,
                device_id=(me_p, other),
                device_id_type=MESH,
            ).start()

        dst[me_c] = src[me_c]

    def wait_spread(buf, sem):
        part = buf.at[pl.ds(0, NC - 1)]
        pltpu.make_async_copy(part, part, sem).wait()

    spread(at_s, at_r, cs_sem.at[0], cr_sem.at[0])

    loads[4].wait()
    loads[5].wait()
    g2 = dot_nt(og[...], o2[...]).astype(BF)
    for g in range(NP):
        gtwo[g] = g2[:, g * LANES : (g + 1) * LANES]
    seg_row = seg[...].astype(F32)
    bias[...] = jnp.where(column(seg_row, R) == seg_row, 0.0, -1e30)

    def arrive(j):
        part = qkv_r.at[j, pl.ds(0, (NP - 1) * R)]
        pltpu.make_async_copy(part, part, xr_sem.at[j]).wait()

    arrive(1)
    arrive(2)
    va[:, :LANES] = qkv_r[2]
    va[:, LANES:] = jnp.ones((KEYS, LANES), BF)
    arrive(0)

    @pl.loop(0, NP)
    def _(k):
        s = lax.rem(me_p + 1 + k, NP)
        rows_s = pl.ds(pl.multiple_of(s * R, R), R)
        qs = qkv_r[0, rows_s, :]
        keys = qkv_r[1]
        mixed = jnp.zeros((R, LANES), F32)
        inv = jnp.zeros((R, LANES), F32)
        for h in range(per):
            mask = head_mask(R, h)
            scores = dot_nt(jnp.where(mask, qs, jnp.zeros((), BF)), keys)
            top = jnp.max(scores, axis=1, keepdims=True)
            e = jnp.exp2(scores - top).astype(BF)
            for t in range(NP):
                ex[h, t, rows_s, :] = e[:, t * R : (t + 1) * R]
            both = dot(e, va[...])
            one = 1.0 / both[:, LANES:]
            mixed = jnp.where(mask, both[:, :LANES] * one, mixed)
            inv = jnp.where(mask, one, inv)
        mix_all[rows_s, :] = mixed
        inv_all[rows_s, :] = inv
        mix_s[s] = mixed.astype(BF)

        @pl.when(k < NP - 1)
        def _():
            pltpu.make_async_remote_copy(
                src_ref=mix_s.at[s],
                dst_ref=mix_r.at[me_p],
                send_sem=ms_sem,
                recv_sem=mr_sem,
                device_id=(s, me_c),
                device_id_type=MESH,
            ).start()

    mix_r[me_p] = mix_s[me_p]

    wait_spread(at_r, cr_sem.at[0])
    landing = at_r[...].reshape(NC, LANES)
    turned = landing.T
    for r in range(CAP):
        p2[:, r * NC : (r + 1) * NC] = jnp.where(
            (iota((R, NC), 0) + 1).astype(F32) == turned[r : r + 1, :], 1.0, 0.0
        ).astype(BF)
        p2t[r * NC : (r + 1) * NC, :] = jnp.where(
            (iota((NC, R), 1) + 1).astype(F32) == landing[:, r : r + 1], 1.0, 0.0
        ).astype(BF)

    part = mix_r.at[pl.ds(0, NP - 1)]
    pltpu.make_async_copy(part, part, mr_sem).wait()
    loads[2].wait()
    mixed = jnp.concatenate([mix_r[p] for p in range(NP)], axis=1)
    moved = (x[...].astype(F32) + dot(mixed, o1[...])).astype(BF)

    chunks = D // LANES
    sub = CAP * chunks

    def pack(choose, what, dst):
        y = dot(choose, what)
        for r in range(CAP):
            for c in range(chunks):
                tmp[pl.ds(c * CAP + r, NC, sub), :] = y[
                    r * NC : (r + 1) * NC, c * LANES : (c + 1) * LANES
                ]
        dst[...] = tmp[...].reshape(NC, sub, LANES).astype(BF)

    def unpack(choose, src):
        tmp[...] = src[...].astype(F32).reshape(NC * sub, LANES)
        got = jnp.concatenate(
            [
                jnp.concatenate([tmp[pl.ds(c * CAP + r, NC, sub), :] for c in range(chunks)], axis=1)
                for r in range(CAP)
            ],
            axis=0,
        ).astype(BF)
        return dot(choose, got)

    pack(pk[...], moved, a_s)
    spread(a_s, a_r, cs_sem.at[1], cr_sem.at[1])
    loads[3].wait()
    wait_spread(a_r, cr_sem.at[1])

    hil[...] = unpack(p2[...], a_r)
    rows = hil[...]
    normed = (rows * norm_scale(rows) * gain2[...]).astype(BF)
    for j in range(3):
        part = dot(normed, w2[:, j * D : (j + 1) * D])
        part = (part * to_log2 if j == 0 else part).astype(BF)
        for g in range(NP):
            two[j, g] = part[:, g * LANES : (g + 1) * LANES]

    @pl.loop(0, NP)
    def _(g):
        qg, kg, vg, gg = two[0, g], two[1, g], two[2, g], gtwo[g].astype(F32)
        va2 = jnp.concatenate([vg, jnp.ones((R, LANES), BF)], axis=1)
        dq = jnp.zeros((R, LANES), F32)
        dk = jnp.zeros((R, LANES), F32)
        dv = jnp.zeros((R, LANES), F32)
        zero = jnp.zeros((), BF)
        for h in range(per):
            mask = head_mask(R, h)
            qh = jnp.where(mask, qg, zero)
            scores = dot_nt(qh, kg) + bias[...]
            e = jnp.exp2(scores - jnp.max(scores, axis=1, keepdims=True)).astype(BF)
            both = dot(e, va2)
            one = 1.0 / both[:, LANES:]
            gi = jnp.where(mask, gg * one, 0.0)
            inner = gi * (both[:, :LANES] * one)
            gib = gi.astype(BF)
            ga = jnp.concatenate([gib, (-inner).astype(BF)], axis=1)
            ds = (e.astype(F32) * dot_nt(ga, va2)).astype(BF)
            dq = dq + dot(ds, jnp.where(mask, kg, zero))
            dk = dk + dot_tn(ds, qh)
            dv = dv + dot_tn(e, gib)
        dtwo[0, g] = (dq * scale).astype(BF)
        dtwo[1, g] = (dk * from_log2).astype(BF)
        dtwo[2, g] = dv.astype(BF)

    def input_grad(d, w):
        total = None
        for j in range(3):
            piece = jnp.concatenate([d[j, g] for g in range(NP)], axis=1)
            term = dot_nt(piece, w[:, j * D : (j + 1) * D])
            total = term if total is None else total + term
        return total.astype(BF).astype(F32)

    path = norm_grad(hil[...], gain2[...], input_grad(dtwo, w2)).astype(BF)
    hil_grad = (og[...].astype(F32) + path.astype(F32)).astype(BF)

    pack(p2t[...], hil_grad, b_s)
    spread(b_s, b_r, cs_sem.at[2], cr_sem.at[2])
    wait_spread(b_r, cr_sem.at[2])
    moved_grad = unpack(gat[...], b_r).astype(BF)
    hil[...] = moved_grad.astype(F32)

    g1 = dot_nt(moved_grad, o1[...]).astype(BF)
    for p in range(NP):
        g_s[p] = g1[:, p * LANES : (p + 1) * LANES]
    for k in range(1, NP):
        pltpu.make_async_remote_copy(
            src_ref=g_s.at[peer(k)],
            dst_ref=g_r.at[my_rows],
            send_sem=gs_sem,
            recv_sem=gr_sem,
            device_id=(peer(k), me_c),
            device_id_type=MESH,
        ).start()
    g_r[my_rows, :] = g_s[me_p]
    part = g_r.at[pl.ds(0, (NP - 1) * R)]
    pltpu.make_async_copy(part, part, gr_sem).wait()

    dq_acc[...] = jnp.zeros((KEYS, LANES), F32)

    @pl.loop(0, NP)
    def _(k):
        t = lax.rem(me_p + 1 + k, NP)
        rows_t = pl.ds(pl.multiple_of(t * R, R), R)
        kt = qkv_r[1, rows_t, :]
        vat = va[rows_t, :]
        zero = jnp.zeros((), BF)
        dk = jnp.zeros((R, LANES), F32)
        dv = jnp.zeros((R, LANES), F32)
        gi = g_r[...].astype(F32) * inv_all[...]
        inner = (-gi * mix_all[...]).astype(BF)
        gi = gi.astype(BF)
        dq = dq_acc[...]
        for h in range(per):
            mask = head_mask(KEYS, h)
            gih = jnp.where(mask, gi, zero)
            ga = jnp.concatenate([gih, jnp.where(mask, inner, zero)], axis=1)
            e = ex[h, t]
            ds = (e.astype(F32) * dot_nt(ga, vat)).astype(BF)
            dq = dq + dot(ds, jnp.where(head_mask(R, h), kt, zero))
            dk = dk + dot_tn(ds, jnp.where(mask, qkv_r[0], zero))
            dv = dv + dot_tn(e, gih)
        dq_acc[...] = dq
        d_s[1, t] = (dk * from_log2).astype(BF)
        d_s[2, t] = dv.astype(BF)

        @pl.when(k < NP - 1)
        def _():
            for j in (1, 2):
                pltpu.make_async_remote_copy(
                    src_ref=d_s.at[j, t],
                    dst_ref=d_r.at[j, me_p],
                    send_sem=ds_sem,
                    recv_sem=dr_sem.at[j],
                    device_id=(t, me_c),
                    device_id_type=MESH,
                ).start()

    for p in range(NP):
        d_s[0, p] = (dq_acc[p * R : (p + 1) * R, :] * scale).astype(BF)
    for k in range(1, NP):
        pltpu.make_async_remote_copy(
            src_ref=d_s.at[0, peer(k)],
            dst_ref=d_r.at[0, me_p],
            send_sem=ds_sem,
            recv_sem=dr_sem.at[0],
            device_id=(peer(k), me_c),
            device_id_type=MESH,
        ).start()
    for j in range(3):
        d_r[j, me_p] = d_s[j, me_p]
    for j in (1, 2, 0):
        part = d_r.at[j, pl.ds(0, NP - 1)]
        pltpu.make_async_copy(part, part, dr_sem.at[j]).wait()

    path = norm_grad(x[...].astype(F32), gain1[...], input_grad(d_r, w1)).astype(BF)
    out[...] = (hil[...] + path.astype(F32)).astype(BF)

    for j in range(3):
        part = qkv_s.at[j, pl.ds(0, NP - 1)]
    part = qkv_s.at[:, pl.ds(0, NP - 1)]
    pltpu.make_async_copy(part, part, xs_sem).wait()
    part = mix_s.at[pl.ds(0, NP - 1)]
    pltpu.make_async_copy(part, part, ms_sem).wait()
    wait_spread(at_s, cs_sem.at[0])
    wait_spread(a_s, cs_sem.at[1])
    wait_spread(b_s, cs_sem.at[2])
    part = g_s.at[pl.ds(0, NP - 1)]
    pltpu.make_async_copy(part, part, gs_sem).wait()
    part = d_s.at[:, pl.ds(0, NP - 1)]
    pltpu.make_async_copy(part, part, ds_sem).wait()


def shards(
    points, norm_gain_one, qkv_one, out_one, hilbert_pos,
    norm_gain_two, qkv_two, out_two, hilbert_seg, out_grad,
):
    R, D = points.shape[2], points.shape[3]
    NP, NC = lax.axis_size("patch"), lax.axis_size("curve")
    DEPTH = D // HEADS
    CAP = 2 * R // NC
    KEYS, SLOTS, chunks = NP * R, CAP * NC, D // LANES
    per = LANES // DEPTH
    sub = CAP * chunks
    vmem = pl.BlockSpec(memory_space=pltpu.VMEM)
    hbm = pl.BlockSpec(memory_space=pl.ANY)
    V = pltpu.VMEM
    DMA = pltpu.SemaphoreType.DMA
    scratch = dict(
        x=V((R, D), BF), w1=V((D, 3 * D), BF), o1=V((D, D), BF), w2=V((D, 3 * D), BF),
        o2=V((D, D), BF), og=V((R, D), BF),
        qkv_s=V((3, NP, R, LANES), BF), qkv_r=V((3, KEYS, LANES), BF),
        va=V((KEYS, 2 * LANES), BF), ex=V((per, NP, KEYS, R), BF),
        inv_all=V((KEYS, LANES), F32), mix_all=V((KEYS, LANES), F32),
        mix_s=V((NP, R, LANES), BF), mix_r=V((NP, R, LANES), BF),
        at_s=V((NC, 1, LANES), F32), at_r=V((NC, 1, LANES), F32),
        tmp=V((NC * sub, LANES), F32),
        a_s=V((NC, sub, LANES), BF), a_r=V((NC, sub, LANES), BF),
        b_s=V((NC, sub, LANES), BF), b_r=V((NC, sub, LANES), BF),
        pk=V((SLOTS, R), BF), gat=V((R, SLOTS), BF), p2=V((R, SLOTS), BF), p2t=V((SLOTS, R), BF),
        bias=V((R, R), F32), hil=V((R, D), F32),
        two=V((3, NP, R, LANES), BF), gtwo=V((NP, R, LANES), BF), dtwo=V((3, NP, R, LANES), BF),
        g_s=V((NP, R, LANES), BF), g_r=V((KEYS, LANES), BF), dq_acc=V((KEYS, LANES), F32),
        d_s=V((3, NP, R, LANES), BF), d_r=V((3, NP, R, LANES), BF),
        lsem=DMA((6,)), xs=DMA, xr=DMA((3,)), ms=DMA, mr=DMA, cs=DMA((3,)), cr=DMA((3,)),
        gs=DMA, gr=DMA, ds=DMA, dr=DMA((3,)),
    )
    result = pl.pallas_call(
        functools.partial(kernel, NP, NC, R, D, CAP, DEPTH),
        out_shape=jax.ShapeDtypeStruct((R, D), BF),
        in_specs=[hbm] * 6 + [vmem] * 4,
        out_specs=vmem,
        scratch_shapes=list(scratch.values()),
        compiler_params=pltpu.CompilerParams(
            collective_id=0, has_side_effects=True, vmem_limit_bytes=56 * 1024 * 1024
        ),
    )(
        points.reshape(R, D), qkv_one, out_one, qkv_two, out_two, out_grad.reshape(R, D),
        norm_gain_one.reshape(1, D), norm_gain_two.reshape(1, D),
        hilbert_pos.reshape(1, R), hilbert_seg.reshape(1, R),
    )
    return result.reshape(points.shape)


def solution(mesh):
    in_specs = (
        P("curve", "patch", None, None), P(), P(), P(), P("curve", "patch", None),
        P(), P(), P(), P("patch", "curve", None), P("patch", "curve", None, None),
    )
    out_specs = P("curve", "patch", None, None)
    return jax.shard_map(shards, mesh=mesh, in_specs=in_specs, out_specs=out_specs, check_vma=False)
```

```python
import functools
import math

import jax
import jax.numpy as jnp
from jax import lax
from jax.experimental import pallas as pl
from jax.experimental.pallas import tpu as pltpu
from jax.sharding import PartitionSpec as P

HEADS = 16
EPS = 1e-06
F32 = jnp.float32
BF = jnp.bfloat16
MESH = pl.DeviceIdType.MESH
LANES = 128


def dot(a, b):
    return lax.dot_general(a, b, (((1,), (0,)), ((), ())), preferred_element_type=F32)


def dot_nt(a, b):
    return lax.dot_general(a, b, (((1,), (1,)), ((), ())), preferred_element_type=F32)


def dot_tn(a, b):
    return lax.dot_general(a, b, (((0,), (0,)), ((), ())), preferred_element_type=F32)


def iota(shape, dim):
    return lax.broadcasted_iota(jnp.int32, shape, dim)


def norm_scale(rows):
    return lax.rsqrt(jnp.mean(rows * rows, axis=-1, keepdims=True) + EPS)


def norm_grad(rows, gain, cot):
    r = norm_scale(rows)
    c = cot * gain
    inner = jnp.mean(c * rows, axis=-1, keepdims=True)
    return r * (c - rows * (r * r * inner))


def column(row, size):
    eye = iota((size, size), 0) == iota((size, size), 1)
    return jnp.sum(jnp.where(eye, row, 0.0), axis=1, keepdims=True)


def kernel(
    NP, NC, R, D, CAP, DEPTH,
    x_hbm, w1_hbm, o1_hbm, w2_hbm, o2_hbm, og_hbm, gain1, gain2, pos, seg,
    out,
    x, w1, o1, w2, o2, og,
    qkv_s, qkv_r, va, ex, inv_all, mix_all,
    mix_s, mix_r, at_s, at_r, tmp, a_s, a_r, b_s, b_r,
    pk, gat, p2, p2t, bias, hil, two, gtwo, dtwo,
    g_s, g_r, dq_acc, d_s, d_r, qm, ga, dk_acc, dv_acc,
    lsem, xs_sem, xr_sem, ms_sem, mr_sem, cs_sem, cr_sem, gs_sem, gr_sem, ds_sem, dr_sem, vouch_sem, xq_sem,
):
    me_p = lax.axis_index("patch")
    me_c = lax.axis_index("curve")
    scale = DEPTH ** (-0.5)
    to_log2 = scale * math.log2(math.e)
    from_log2 = math.log(2.0)
    per = LANES // DEPTH
    KEYS = NP * R
    SLOTS = CAP * NC

    loads = [
        pltpu.make_async_copy(src, dst, lsem.at[i])
        for i, (src, dst) in enumerate(
            [(x_hbm, x), (w1_hbm, w1), (o1_hbm, o1), (w2_hbm, w2), (o2_hbm, o2), (og_hbm, og)]
        )
    ]
    for load in loads:
        load.start()

    barrier = pltpu.get_barrier_semaphore()

    def peer(k):
        return lax.rem(me_p + k, NP)

    inner = 1 << (NC.bit_length() // 2)
    outer = NC // inner
    row, place_in = me_c // inner, lax.rem(me_c, inner)
    beside = [
        (me_p, lax.rem(row + k, outer) * inner + place_in)
        for k in ((1, outer - 1) if outer > 2 else (1,))
    ]
    greeted = [(peer(k), me_c) for k in range(1, NP)]
    greeted += [(me_p, row * inner + lax.rem(place_in + k, inner)) for k in range(1, inner)]
    greeted += beside
    for device in greeted:
        pl.semaphore_signal(barrier, inc=1, device_id=device, device_id_type=MESH)

    def vouch(i):
        for device in beside:
            pl.semaphore_signal(vouch_sem.at[i], inc=1, device_id=device, device_id_type=MESH)

    def vouched(i):
        pl.semaphore_wait(vouch_sem.at[i], len(beside))

    rounds = outer // 2

    def head_mask(rows, h):
        return iota((rows, LANES), 1) // DEPTH == h

    loads[0].wait()
    loads[1].wait()
    rows = x[...].astype(F32)
    normed = (rows * norm_scale(rows) * gain1[...]).astype(BF)
    for j in (1, 2, 0):
        part = dot(normed, w1[:, j * D : (j + 1) * D])
        part = (part * to_log2 if j == 0 else part).astype(BF)
        for p in range(NP):
            qkv_s[j, p] = part[:, p * LANES : (p + 1) * LANES]

    pl.semaphore_wait(barrier, len(greeted))

    def far(k):
        return pl.ds((NP - k) % NP * R, R)

    for j in (1, 2, 0):
        for k in range(1, NP):
            pltpu.make_async_remote_copy(
                src_ref=qkv_s.at[j, peer(k)],
                dst_ref=qkv_r.at[j, far(k)],
                send_sem=xs_sem,
                recv_sem=xr_sem.at[j] if j else xq_sem.at[NP - k],
                device_id=(peer(k), me_c),
                device_id_type=MESH,
            ).start()
        qkv_r[j, far(0), :] = qkv_s[j, me_p]
    vouch(0)

    place = pos[...]
    owner_row = (place // R).astype(F32)
    offset_row = (place % R).astype(F32)
    owner_col = column(owner_row, R)
    offset_col = column(offset_row, R)
    same = owner_col == owner_row
    i0, i1 = iota((R, R), 0), iota((R, R), 1)
    rank_row = jnp.sum(jnp.where(same & (i0 < i1), 1.0, 0.0), axis=0, keepdims=True)
    rank_col = jnp.sum(jnp.where(same & (i1 < i0), 1.0, 0.0), axis=1, keepdims=True)
    slot_row = rank_row * NC + owner_row
    slot_col = rank_col * NC + owner_col
    pk[...] = jnp.where(iota((SLOTS, R), 0).astype(F32) == slot_row, 1.0, 0.0).astype(BF)
    gat[...] = jnp.where(iota((R, SLOTS), 1).astype(F32) == slot_col, 1.0, 0.0).astype(BF)
    table = dot(pk[...], jnp.broadcast_to(offset_col + 1.0, (R, LANES)).astype(BF))
    lane = iota((NC, LANES), 1)
    note = jnp.zeros((NC, LANES), F32)
    for r in range(CAP):
        note = jnp.where(lane == r, table[r * NC : (r + 1) * NC], note)
    at_s[...] = note.reshape(NC, 1, LANES)

    def spread(src, dst, send_sem, recv_sem):
        @pl.loop(1, NC)
        def _(k):
            other = lax.rem(me_c + lax.rem(k * 51, NC), NC)
            pltpu.make_async_remote_copy(
                src_ref=src.at[other],
                dst_ref=dst.at[me_c],
                send_sem=send_sem,
                recv_sem=recv_sem,
                device_id=(me_p, other),
                device_id_type=MESH,
            ).start()

        dst[me_c] = src[me_c]

    def wait_spread(buf, sem):
        part = buf.at[pl.ds(0, NC - 1)]
        pltpu.make_async_copy(part, part, sem).wait()

    loads[4].wait()
    loads[5].wait()
    g2 = dot_nt(og[...], o2[...]).astype(BF)
    for g in range(NP):
        gtwo[g] = g2[:, g * LANES : (g + 1) * LANES]
    seg_row = seg[...].astype(F32)
    bias[...] = jnp.where(column(seg_row, R) == seg_row, 0.0, -1e30)
    for i in range(rounds):
        vouched(i)
        if i + 1 < rounds:
            vouch(i + 1)
    spread(at_s, at_r, cs_sem.at[0], cr_sem.at[0])


    def arrive(j):
        part = qkv_r.at[j, pl.ds(0, (NP - 1) * R)]
        pltpu.make_async_copy(part, part, xr_sem.at[j]).wait()

    arrive(1)
    arrive(2)
    va[:, :LANES] = qkv_r[2]
    va[:, LANES:] = jnp.ones((KEYS, LANES), BF)

    @pl.loop(0, NP)
    def _(s):
        rows_s = pl.ds(pl.multiple_of(s * R, R), R)

        @pl.when(s > 0)
        def _():
            part = qkv_r.at[0, rows_s]
            pltpu.make_async_copy(part, part, xq_sem.at[s]).wait()

        qs = qkv_r[0, rows_s, :]
        keys = qkv_r[1]
        mixed = jnp.zeros((R, LANES), F32)
        inv = jnp.zeros((R, LANES), F32)
        for h in range(per):
            mask = head_mask(R, h)
            qh = jnp.where(mask, qs, jnp.zeros((), BF))
            qm[h, rows_s, :] = qh
            scores = dot_nt(qh, keys)
            top = jnp.max(scores, axis=1, keepdims=True)
            e = jnp.exp2(scores - top).astype(BF)
            for t in range(NP):
                ex[h, t, rows_s, :] = e[:, t * R : (t + 1) * R]
            both = dot(e, va[...])
            one = 1.0 / both[:, LANES:]
            mixed = jnp.where(mask, both[:, :LANES] * one, mixed)
            inv = jnp.where(mask, one, inv)
        mix_all[rows_s, :] = mixed
        inv_all[rows_s, :] = inv
        mix_s[s] = mixed.astype(BF)

        @pl.when(s > 0)
        def _():
            pltpu.make_async_remote_copy(
                src_ref=mix_s.at[s],
                dst_ref=mix_r.at[me_p],
                send_sem=ms_sem,
                recv_sem=mr_sem,
                device_id=(peer(s), me_c),
                device_id_type=MESH,
            ).start()

    mix_r[me_p] = mix_s[0]

    wait_spread(at_r, cr_sem.at[0])
    landing = at_r[...].reshape(NC, LANES)
    turned = landing.T
    for r in range(CAP):
        p2[:, r * NC : (r + 1) * NC] = jnp.where(
            (iota((R, NC), 0) + 1).astype(F32) == turned[r : r + 1, :], 1.0, 0.0
        ).astype(BF)
        p2t[r * NC : (r + 1) * NC, :] = jnp.where(
            (iota((NC, R), 1) + 1).astype(F32) == landing[:, r : r + 1], 1.0, 0.0
        ).astype(BF)

    part = mix_r.at[pl.ds(0, NP - 1)]
    pltpu.make_async_copy(part, part, mr_sem).wait()
    loads[2].wait()
    mixed = jnp.concatenate([mix_r[p] for p in range(NP)], axis=1)
    moved = (x[...].astype(F32) + dot(mixed, o1[...])).astype(BF)

    chunks = D // LANES
    sub = CAP * chunks

    def pack(choose, what, dst):
        y = dot(choose, what)
        for r in range(CAP):
            for c in range(chunks):
                tmp[pl.ds(c * CAP + r, NC, sub), :] = y[
                    r * NC : (r + 1) * NC, c * LANES : (c + 1) * LANES
                ]
        dst[...] = tmp[...].reshape(NC, sub, LANES).astype(BF)

    def unpack(choose, src):
        tmp[...] = src[...].astype(F32).reshape(NC * sub, LANES)
        got = jnp.concatenate(
            [
                jnp.concatenate([tmp[pl.ds(c * CAP + r, NC, sub), :] for c in range(chunks)], axis=1)
                for r in range(CAP)
            ],
            axis=0,
        ).astype(BF)
        return dot(choose, got)

    pack(pk[...], moved, a_s)
    spread(a_s, a_r, cs_sem.at[1], cr_sem.at[1])
    loads[3].wait()
    wait_spread(a_r, cr_sem.at[1])

    hil[...] = unpack(p2[...], a_r)
    rows = hil[...]
    normed = (rows * norm_scale(rows) * gain2[...]).astype(BF)
    for j in range(3):
        part = dot(normed, w2[:, j * D : (j + 1) * D])
        part = (part * to_log2 if j == 0 else part).astype(BF)
        for g in range(NP):
            two[j, g] = part[:, g * LANES : (g + 1) * LANES]

    def stack(m):
        zero = jnp.zeros((), m.dtype)
        return jnp.concatenate([jnp.where(head_mask(R, h), m, zero) for h in range(per)], axis=0)

    for g in range(NP):
        qg, kg, vg = stack(two[0, g]), two[1, g], two[2, g]
        va2 = jnp.concatenate([vg, jnp.ones((R, LANES), BF)], axis=1)
        scores = dot_nt(qg, kg) + jnp.concatenate([bias[...]] * per, axis=0)
        e = jnp.exp2(scores - jnp.max(scores, axis=1, keepdims=True)).astype(BF)
        both = dot(e, va2)
        one = 1.0 / both[:, LANES:]
        gi = stack(gtwo[g].astype(F32)) * one
        less = -gi * (both[:, :LANES] * one)
        gib = gi.astype(BF)
        lhs = jnp.concatenate([gib, less.astype(BF)], axis=1)
        ds = (e.astype(F32) * dot_nt(lhs, va2)).astype(BF)
        full = dot(ds, kg)
        dq = full[:R]
        for h in range(1, per):
            dq = jnp.where(head_mask(R, h), full[h * R : (h + 1) * R], dq)
        dtwo[0, g] = (dq * scale).astype(BF)
        dtwo[1, g] = (dot_tn(ds, qg) * from_log2).astype(BF)
        dtwo[2, g] = dot_tn(e, gib).astype(BF)

    def input_term(d, w, j):
        piece = jnp.concatenate([d[j, g] for g in range(NP)], axis=1)
        return dot_nt(piece, w[:, j * D : (j + 1) * D])

    def input_grad(d, w):
        total = input_term(d, w, 0) + input_term(d, w, 1) + input_term(d, w, 2)
        return total.astype(BF).astype(F32)

    path = norm_grad(hil[...], gain2[...], input_grad(dtwo, w2)).astype(BF)
    hil_grad = (og[...].astype(F32) + path.astype(F32)).astype(BF)

    pack(p2t[...], hil_grad, b_s)
    spread(b_s, b_r, cs_sem.at[2], cr_sem.at[2])
    wait_spread(b_r, cr_sem.at[2])
    moved_grad = unpack(gat[...], b_r).astype(BF)
    hil[...] = moved_grad.astype(F32)

    g1 = dot_nt(moved_grad, o1[...]).astype(BF)
    for p in range(NP):
        g_s[p] = g1[:, p * LANES : (p + 1) * LANES]
    for k in range(1, NP):
        pltpu.make_async_remote_copy(
            src_ref=g_s.at[peer(k)],
            dst_ref=g_r.at[far(k)],
            send_sem=gs_sem,
            recv_sem=gr_sem,
            device_id=(peer(k), me_c),
            device_id_type=MESH,
        ).start()
    g_r[far(0), :] = g_s[me_p]

    def scaled(lo, count):
        here = slice(lo, lo + count)
        gi = g_r[here, :].astype(F32) * inv_all[here, :]
        less = (-gi * mix_all[here, :]).astype(BF)
        gi = gi.astype(BF)
        zero = jnp.zeros((), BF)
        for h in range(per):
            mask = head_mask(count, h)
            ga[h, here, :LANES] = jnp.where(mask, gi, zero)
            ga[h, here, LANES:] = jnp.where(mask, less, zero)

    def pair(lo, count, t):
        here = slice(lo, lo + count)
        rows_t = pl.ds(pl.multiple_of(t * R, R), R) if not isinstance(t, int) else pl.ds(t * R, R)
        kt = qkv_r[1, rows_t, :]
        vat = va[rows_t, :]
        dq = dk = dv = None
        for h in range(per):
            gah = ga[h, here, :]
            e = ex[h, t, here, :]
            ds = (e.astype(F32) * dot_nt(gah, vat)).astype(BF)
            q_term = dot(ds, jnp.where(head_mask(R, h), kt, jnp.zeros((), BF)))
            k_term = dot_tn(ds, qm[h, here, :])
            v_term = dot_tn(e, gah[:, :LANES])
            dq = q_term if dq is None else dq + q_term
            dk = k_term if dk is None else dk + k_term
            dv = v_term if dv is None else dv + v_term
        return dq, dk, dv

    scaled(0, R)
    dq_acc[...] = jnp.zeros((KEYS, LANES), F32)

    @pl.loop(1, NP)
    def _(t):
        dq, dk, dv = pair(0, R, t)
        dq_acc[:R] += dq
        dk_acc[t] = dk
        dv_acc[t] = dv

    part = g_r.at[pl.ds(0, (NP - 1) * R)]
    pltpu.make_async_copy(part, part, gr_sem).wait()
    scaled(R, (NP - 1) * R)
    dk_acc[0] = jnp.zeros((R, LANES), F32)
    dv_acc[0] = jnp.zeros((R, LANES), F32)

    @pl.loop(1, NP + 1)
    def _(i):
        t = lax.rem(i, NP)
        dq, dk, dv = pair(R, (NP - 1) * R, t)
        dq_acc[R:] += dq
        dk = dk_acc[t] + dk
        dv = dv_acc[t] + dv

        @pl.when(i == NP)
        def _():
            dk_acc[0] = dk
            dv_acc[0] = dv

        @pl.when(i < NP)
        def _():
            d_s[1, t] = (dk * from_log2).astype(BF)
            d_s[2, t] = dv.astype(BF)
            for j in (1, 2):
                pltpu.make_async_remote_copy(
                    src_ref=d_s.at[j, t],
                    dst_ref=d_r.at[j, me_p],
                    send_sem=ds_sem,
                    recv_sem=dr_sem.at[j],
                    device_id=(peer(t), me_c),
                    device_id_type=MESH,
                ).start()

    for k in range(1, NP):
        d_s[0, k] = (dq_acc[k * R : (k + 1) * R, :] * scale).astype(BF)
        pltpu.make_async_remote_copy(
            src_ref=d_s.at[0, k],
            dst_ref=d_r.at[0, me_p],
            send_sem=ds_sem,
            recv_sem=dr_sem.at[0],
            device_id=(peer(k), me_c),
            device_id_type=MESH,
        ).start()

    dq, dk, dv = pair(0, R, 0)
    d_r[0, me_p] = ((dq_acc[:R] + dq) * scale).astype(BF)
    d_r[1, me_p] = ((dk_acc[0] + dk) * from_log2).astype(BF)
    d_r[2, me_p] = (dv_acc[0] + dv).astype(BF)

    def landed(j):
        part = d_r.at[j, pl.ds(0, NP - 1)]
        pltpu.make_async_copy(part, part, dr_sem.at[j]).wait()

    landed(1)
    landed(2)
    total = input_term(d_r, w1, 1) + input_term(d_r, w1, 2)
    landed(0)
    total = (total + input_term(d_r, w1, 0)).astype(BF).astype(F32)
    path = norm_grad(x[...].astype(F32), gain1[...], total).astype(BF)
    out[...] = (hil[...] + path.astype(F32)).astype(BF)

    part = qkv_s.at[:, pl.ds(0, NP - 1)]
    pltpu.make_async_copy(part, part, xs_sem).wait()
    part = mix_s.at[pl.ds(0, NP - 1)]
    pltpu.make_async_copy(part, part, ms_sem).wait()
    wait_spread(at_s, cs_sem.at[0])
    wait_spread(a_s, cs_sem.at[1])
    wait_spread(b_s, cs_sem.at[2])
    part = g_s.at[pl.ds(0, NP - 1)]
    pltpu.make_async_copy(part, part, gs_sem).wait()
    part = d_s.at[:, pl.ds(0, NP - 1)]
    pltpu.make_async_copy(part, part, ds_sem).wait()


def shards(
    points, norm_gain_one, qkv_one, out_one, hilbert_pos,
    norm_gain_two, qkv_two, out_two, hilbert_seg, out_grad,
):
    R, D = points.shape[2], points.shape[3]
    NP, NC = lax.axis_size("patch"), lax.axis_size("curve")
    DEPTH = D // HEADS
    CAP = 2 * R // NC
    KEYS, SLOTS, chunks = NP * R, CAP * NC, D // LANES
    per = LANES // DEPTH
    sub = CAP * chunks
    vmem = pl.BlockSpec(memory_space=pltpu.VMEM)
    hbm = pl.BlockSpec(memory_space=pl.ANY)
    V = pltpu.VMEM
    DMA = pltpu.SemaphoreType.DMA
    scratch = dict(
        x=V((R, D), BF), w1=V((D, 3 * D), BF), o1=V((D, D), BF), w2=V((D, 3 * D), BF),
        o2=V((D, D), BF), og=V((R, D), BF),
        qkv_s=V((3, NP, R, LANES), BF), qkv_r=V((3, KEYS, LANES), BF),
        va=V((KEYS, 2 * LANES), BF), ex=V((per, NP, KEYS, R), BF),
        inv_all=V((KEYS, LANES), F32), mix_all=V((KEYS, LANES), F32),
        mix_s=V((NP, R, LANES), BF), mix_r=V((NP, R, LANES), BF),
        at_s=V((NC, 1, LANES), F32), at_r=V((NC, 1, LANES), F32),
        tmp=V((NC * sub, LANES), F32),
        a_s=V((NC, sub, LANES), BF), a_r=V((NC, sub, LANES), BF),
        b_s=V((NC, sub, LANES), BF), b_r=V((NC, sub, LANES), BF),
        pk=V((SLOTS, R), BF), gat=V((R, SLOTS), BF), p2=V((R, SLOTS), BF), p2t=V((SLOTS, R), BF),
        bias=V((R, R), F32), hil=V((R, D), F32),
        two=V((3, NP, R, LANES), BF), gtwo=V((NP, R, LANES), BF), dtwo=V((3, NP, R, LANES), BF),
        g_s=V((NP, R, LANES), BF), g_r=V((KEYS, LANES), BF), dq_acc=V((KEYS, LANES), F32),
        d_s=V((3, NP, R, LANES), BF), d_r=V((3, NP, R, LANES), BF),
        qm=V((per, KEYS, LANES), BF), ga=V((per, KEYS, 2 * LANES), BF),
        dk_acc=V((NP, R, LANES), F32), dv_acc=V((NP, R, LANES), F32),
        lsem=DMA((6,)), xs=DMA, xr=DMA((3,)), ms=DMA, mr=DMA, cs=DMA((3,)), cr=DMA((3,)),
        gs=DMA, gr=DMA, ds=DMA, dr=DMA((3,)), vouch=pltpu.SemaphoreType.REGULAR((8,)), xq=DMA((NP,)),
    )
    result = pl.pallas_call(
        functools.partial(kernel, NP, NC, R, D, CAP, DEPTH),
        out_shape=jax.ShapeDtypeStruct((R, D), BF),
        in_specs=[hbm] * 6 + [vmem] * 4,
        out_specs=vmem,
        scratch_shapes=list(scratch.values()),
        compiler_params=pltpu.CompilerParams(
            collective_id=0, has_side_effects=True, vmem_limit_bytes=56 * 1024 * 1024
        ),
    )(
        points.reshape(R, D), qkv_one, out_one, qkv_two, out_two, out_grad.reshape(R, D),
        norm_gain_one.reshape(1, D), norm_gain_two.reshape(1, D),
        hilbert_pos.reshape(1, R), hilbert_seg.reshape(1, R),
    )
    return result.reshape(points.shape)


def solution(mesh):
    in_specs = (
        P("curve", "patch", None, None), P(), P(), P(), P("curve", "patch", None),
        P(), P(), P(), P("patch", "curve", None), P("patch", "curve", None, None),
    )
    out_specs = P("curve", "patch", None, None)
    return jax.shard_map(shards, mesh=mesh, in_specs=in_specs, out_specs=out_specs, check_vma=False)
```

```python
import functools
import math

import jax
import jax.numpy as jnp
from jax import lax
from jax.experimental import pallas as pl
from jax.experimental.pallas import tpu as pltpu
from jax.sharding import PartitionSpec as P

HEADS = 16
EPS = 1e-06
F32 = jnp.float32
BF = jnp.bfloat16
MESH = pl.DeviceIdType.MESH
LANES = 128


def dot(a, b):
    return lax.dot_general(a, b, (((1,), (0,)), ((), ())), preferred_element_type=F32)


def dot_nt(a, b):
    return lax.dot_general(a, b, (((1,), (1,)), ((), ())), preferred_element_type=F32)


def dot_tn(a, b):
    return lax.dot_general(a, b, (((0,), (0,)), ((), ())), preferred_element_type=F32)


def iota(shape, dim):
    return lax.broadcasted_iota(jnp.int32, shape, dim)


def norm_scale(rows):
    return lax.rsqrt(jnp.mean(rows * rows, axis=-1, keepdims=True) + EPS)


def norm_grad(rows, gain, cot):
    r = norm_scale(rows)
    c = cot * gain
    inner = jnp.mean(c * rows, axis=-1, keepdims=True)
    return r * (c - rows * (r * r * inner))


def column(row, size):
    eye = iota((size, size), 0) == iota((size, size), 1)
    return jnp.sum(jnp.where(eye, row, 0.0), axis=1, keepdims=True)


def kernel(
    NP, NC, R, D, CAP, DEPTH,
    x_hbm, w1_hbm, o1_hbm, w2_hbm, o2_hbm, og_hbm, gain1, gain2, pos, seg,
    out,
    x, w1, o1, w2, o2, og,
    qkv_s, qkv_r, va, ex, inv_all, mix_all,
    mix_s, mix_r, at_s, at_m, at_n, at_r, tmp, a_s, a_r, b_s, b_r,
    pk, gat, p2, p2t, bias, hil, two, gtwo, dtwo,
    g_s, g_r, dq_acc, d_s, d_r, qm, ga, dk_acc, dv_acc,
    lsem, xs_sem, xr_sem, ms_sem, mr_sem, cs_sem, cr_sem, gs_sem, gr_sem, ds_sem, dr_sem, ns_sem, nr_sem, xq_sem,
):
    me_p = lax.axis_index("patch")
    me_c = lax.axis_index("curve")
    scale = DEPTH ** (-0.5)
    to_log2 = scale * math.log2(math.e)
    from_log2 = math.log(2.0)
    per = LANES // DEPTH
    KEYS = NP * R
    SLOTS = CAP * NC

    thirds = [pl.ds(j * D, D) for j in range(3)]
    moves = [(x_hbm, x)] + [(w1_hbm.at[:, thirds[j]], w1.at[:, thirds[j]]) for j in range(3)]
    moves += [(o1_hbm, o1), (w2_hbm, w2), (o2_hbm, o2), (og_hbm, og)]
    loads = [pltpu.make_async_copy(src, dst, lsem.at[i]) for i, (src, dst) in enumerate(moves)]
    for i in (0, 2, 3, 1):
        loads[i].start()

    barrier = pltpu.get_barrier_semaphore()

    def peer(k):
        return lax.rem(me_p + k, NP)

    inner = 1 << (NC.bit_length() // 2)
    outer = NC // inner
    row, place_in = me_c // inner, lax.rem(me_c, inner)
    greeted = [(peer(k), me_c) for k in range(1, NP)]
    greeted += [(me_p, row * inner + lax.rem(place_in + k, inner)) for k in range(1, inner)]
    greeted += [(me_p, lax.rem(row + k, outer) * inner + place_in) for k in range(1, outer)]
    for device in greeted:
        pl.semaphore_signal(barrier, inc=1, device_id=device, device_id_type=MESH)

    def head_mask(rows, h):
        return iota((rows, LANES), 1) // DEPTH == h

    def far(k):
        return pl.ds((NP - k) % NP * R, R)

    loads[0].wait()
    rows = x[...].astype(F32)
    normed = (rows * norm_scale(rows) * gain1[...]).astype(BF)
    for j in (1, 2, 0):
        loads[1 + j].wait()
        part = dot(normed, w1[:, j * D : (j + 1) * D])
        part = (part * to_log2 if j == 0 else part).astype(BF)
        for p in range(NP):
            qkv_s[j, p] = part[:, p * LANES : (p + 1) * LANES]
        if j == 1:
            pl.semaphore_wait(barrier, len(greeted))
        for k in range(1, NP):
            pltpu.make_async_remote_copy(
                src_ref=qkv_s.at[j, peer(k)],
                dst_ref=qkv_r.at[j, far(k)],
                send_sem=xs_sem,
                recv_sem=xr_sem.at[j] if j else xq_sem.at[NP - k],
                device_id=(peer(k), me_c),
                device_id_type=MESH,
            ).start()
        qkv_r[j, far(0), :] = qkv_s[j, me_p]
    for load in loads[4:]:
        load.start()

    place = pos[...]
    owner_row = (place // R).astype(F32)
    offset_row = (place % R).astype(F32)
    owner_col = column(owner_row, R)
    offset_col = column(offset_row, R)
    same = owner_col == owner_row
    i0, i1 = iota((R, R), 0), iota((R, R), 1)
    rank_row = jnp.sum(jnp.where(same & (i0 < i1), 1.0, 0.0), axis=0, keepdims=True)
    rank_col = jnp.sum(jnp.where(same & (i1 < i0), 1.0, 0.0), axis=1, keepdims=True)
    slot_row = rank_row * NC + owner_row
    slot_col = rank_col * NC + owner_col
    pk[...] = jnp.where(iota((SLOTS, R), 0).astype(F32) == slot_row, 1.0, 0.0).astype(BF)
    gat[...] = jnp.where(iota((R, SLOTS), 1).astype(F32) == slot_col, 1.0, 0.0).astype(BF)
    table = dot(pk[...], jnp.broadcast_to(offset_col + 1.0, (R, LANES)).astype(BF))
    lane = iota((NC, LANES), 1)
    note = jnp.zeros((NC, LANES), F32)
    for r in range(CAP):
        note = jnp.where(lane == r, table[r * NC : (r + 1) * NC], note)
    for z in range(outer):
        at_s[pl.ds(z, inner, outer), :] = note[z * inner : (z + 1) * inner]

    def line(k, count, at):
        return pl.ds(pl.multiple_of(lax.rem(at + k, count) * (NC // count), NC // count), NC // count)

    for k in range(1, inner):
        pltpu.make_async_remote_copy(
            src_ref=at_s.at[line(k, inner, place_in)],
            dst_ref=at_m.at[line(0, inner, place_in)],
            send_sem=cs_sem.at[0],
            recv_sem=cr_sem.at[0],
            device_id=(me_p, row * inner + lax.rem(place_in + k, inner)),
            device_id_type=MESH,
        ).start()
    at_m[line(0, inner, place_in), :] = at_s[line(0, inner, place_in), :]

    def spread(src, dst, send_sem, recv_sem):
        @pl.loop(1, NC)
        def _(k):
            other = lax.rem(me_c + lax.rem(k * 51, NC), NC)
            pltpu.make_async_remote_copy(
                src_ref=src.at[other],
                dst_ref=dst.at[me_c],
                send_sem=send_sem,
                recv_sem=recv_sem,
                device_id=(me_p, other),
                device_id_type=MESH,
            ).start()

        dst[me_c] = src[me_c]

    def wait_spread(buf, sem):
        part = buf.at[pl.ds(0, NC - 1)]
        pltpu.make_async_copy(part, part, sem).wait()

    loads[6].wait()
    loads[7].wait()
    g2 = dot_nt(og[...], o2[...]).astype(BF)
    for g in range(NP):
        gtwo[g] = g2[:, g * LANES : (g + 1) * LANES]
    seg_row = seg[...].astype(F32)
    bias[...] = jnp.where(column(seg_row, R) == seg_row, 0.0, -1e30)
    part = at_m.at[pl.ds(0, (inner - 1) * outer)]
    pltpu.make_async_copy(part, part, cr_sem.at[0]).wait()
    for z in range(outer):
        at_n[z * inner : (z + 1) * inner, :] = at_m[pl.ds(z, inner, outer), :]
    for k in range(1, outer):
        pltpu.make_async_remote_copy(
            src_ref=at_n.at[line(k, outer, row)],
            dst_ref=at_r.at[line(0, outer, row)],
            send_sem=ns_sem,
            recv_sem=nr_sem,
            device_id=(me_p, lax.rem(row + k, outer) * inner + place_in),
            device_id_type=MESH,
        ).start()
    at_r[line(0, outer, row), :] = at_n[line(0, outer, row), :]

    def arrive(j):
        part = qkv_r.at[j, pl.ds(0, (NP - 1) * R)]
        pltpu.make_async_copy(part, part, xr_sem.at[j]).wait()

    arrive(1)
    arrive(2)
    va[:, :LANES] = qkv_r[2]
    va[:, LANES:] = jnp.ones((KEYS, LANES), BF)

    @pl.loop(0, NP)
    def _(s):
        rows_s = pl.ds(pl.multiple_of(s * R, R), R)

        @pl.when(s > 0)
        def _():
            part = qkv_r.at[0, rows_s]
            pltpu.make_async_copy(part, part, xq_sem.at[s]).wait()

        qs = qkv_r[0, rows_s, :]
        keys = qkv_r[1]
        mixed = jnp.zeros((R, LANES), F32)
        inv = jnp.zeros((R, LANES), F32)
        for h in range(per):
            mask = head_mask(R, h)
            qh = jnp.where(mask, qs, jnp.zeros((), BF))
            qm[h, rows_s, :] = qh
            scores = dot_nt(qh, keys)
            top = jnp.max(scores, axis=1, keepdims=True)
            e = jnp.exp2(scores - top).astype(BF)
            for t in range(NP):
                ex[h, t, rows_s, :] = e[:, t * R : (t + 1) * R]
            both = dot(e, va[...])
            one = 1.0 / both[:, LANES:]
            mixed = jnp.where(mask, both[:, :LANES] * one, mixed)
            inv = jnp.where(mask, one, inv)
        mix_all[rows_s, :] = mixed
        inv_all[rows_s, :] = inv
        mix_s[s] = mixed.astype(BF)

        @pl.when(s > 0)
        def _():
            pltpu.make_async_remote_copy(
                src_ref=mix_s.at[s],
                dst_ref=mix_r.at[me_p],
                send_sem=ms_sem,
                recv_sem=mr_sem,
                device_id=(peer(s), me_c),
                device_id_type=MESH,
            ).start()

    mix_r[me_p] = mix_s[0]

    part = mix_r.at[pl.ds(0, NP - 1)]
    pltpu.make_async_copy(part, part, mr_sem).wait()
    loads[4].wait()
    mixed = jnp.concatenate([mix_r[p] for p in range(NP)], axis=1)
    moved = (x[...].astype(F32) + dot(mixed, o1[...])).astype(BF)

    chunks = D // LANES
    sub = CAP * chunks

    def pack(choose, what, dst):
        y = dot(choose, what)
        for r in range(CAP):
            for c in range(chunks):
                tmp[pl.ds(c * CAP + r, NC, sub), :] = y[
                    r * NC : (r + 1) * NC, c * LANES : (c + 1) * LANES
                ]
        dst[...] = tmp[...].reshape(NC, sub, LANES).astype(BF)

    def unpack(choose, src):
        tmp[...] = src[...].astype(F32).reshape(NC * sub, LANES)
        got = jnp.concatenate(
            [
                jnp.concatenate([tmp[pl.ds(c * CAP + r, NC, sub), :] for c in range(chunks)], axis=1)
                for r in range(CAP)
            ],
            axis=0,
        ).astype(BF)
        return dot(choose, got)

    pack(pk[...], moved, a_s)
    part = at_r.at[pl.ds(0, (outer - 1) * inner)]
    pltpu.make_async_copy(part, part, nr_sem).wait()
    spread(a_s, a_r, cs_sem.at[1], cr_sem.at[1])

    landing = at_r[...]
    turned = landing.T
    for r in range(CAP):
        p2[:, r * NC : (r + 1) * NC] = jnp.where(
            (iota((R, NC), 0) + 1).astype(F32) == turned[r : r + 1, :], 1.0, 0.0
        ).astype(BF)
        p2t[r * NC : (r + 1) * NC, :] = jnp.where(
            (iota((NC, R), 1) + 1).astype(F32) == landing[:, r : r + 1], 1.0, 0.0
        ).astype(BF)

    loads[5].wait()
    wait_spread(a_r, cr_sem.at[1])

    hil[...] = unpack(p2[...], a_r)
    rows = hil[...]
    normed = (rows * norm_scale(rows) * gain2[...]).astype(BF)
    for j in range(3):
        part = dot(normed, w2[:, j * D : (j + 1) * D])
        part = (part * to_log2 if j == 0 else part).astype(BF)
        for g in range(NP):
            two[j, g] = part[:, g * LANES : (g + 1) * LANES]

    def stack(m):
        zero = jnp.zeros((), m.dtype)
        return jnp.concatenate([jnp.where(head_mask(R, h), m, zero) for h in range(per)], axis=0)

    for g in range(NP):
        qg, kg, vg = stack(two[0, g]), two[1, g], two[2, g]
        va2 = jnp.concatenate([vg, jnp.ones((R, LANES), BF)], axis=1)
        scores = dot_nt(qg, kg) + jnp.concatenate([bias[...]] * per, axis=0)
        e = jnp.exp2(scores - jnp.max(scores, axis=1, keepdims=True)).astype(BF)
        both = dot(e, va2)
        one = 1.0 / both[:, LANES:]
        gi = stack(gtwo[g].astype(F32)) * one
        less = -gi * (both[:, :LANES] * one)
        gib = gi.astype(BF)
        lhs = jnp.concatenate([gib, less.astype(BF)], axis=1)
        ds = (e.astype(F32) * dot_nt(lhs, va2)).astype(BF)
        full = dot(ds, kg)
        dq = full[:R]
        for h in range(1, per):
            dq = jnp.where(head_mask(R, h), full[h * R : (h + 1) * R], dq)
        dtwo[0, g] = (dq * scale).astype(BF)
        dtwo[1, g] = (dot_tn(ds, qg) * from_log2).astype(BF)
        dtwo[2, g] = dot_tn(e, gib).astype(BF)

    def input_term(d, w, j):
        piece = jnp.concatenate([d[j, g] for g in range(NP)], axis=1)
        return dot_nt(piece, w[:, j * D : (j + 1) * D])

    def input_grad(d, w):
        total = input_term(d, w, 0) + input_term(d, w, 1) + input_term(d, w, 2)
        return total.astype(BF).astype(F32)

    path = norm_grad(hil[...], gain2[...], input_grad(dtwo, w2)).astype(BF)
    hil_grad = (og[...].astype(F32) + path.astype(F32)).astype(BF)

    pack(p2t[...], hil_grad, b_s)
    spread(b_s, b_r, cs_sem.at[2], cr_sem.at[2])
    wait_spread(b_r, cr_sem.at[2])
    moved_grad = unpack(gat[...], b_r).astype(BF)
    hil[...] = moved_grad.astype(F32)

    g1 = dot_nt(moved_grad, o1[...]).astype(BF)
    for p in range(NP):
        g_s[p] = g1[:, p * LANES : (p + 1) * LANES]
    for k in range(1, NP):
        pltpu.make_async_remote_copy(
            src_ref=g_s.at[peer(k)],
            dst_ref=g_r.at[far(k)],
            send_sem=gs_sem,
            recv_sem=gr_sem,
            device_id=(peer(k), me_c),
            device_id_type=MESH,
        ).start()
    g_r[far(0), :] = g_s[me_p]

    def scaled(lo, count):
        here = slice(lo, lo + count)
        gi = g_r[here, :].astype(F32) * inv_all[here, :]
        less = (-gi * mix_all[here, :]).astype(BF)
        gi = gi.astype(BF)
        zero = jnp.zeros((), BF)
        for h in range(per):
            mask = head_mask(count, h)
            ga[h, here, :LANES] = jnp.where(mask, gi, zero)
            ga[h, here, LANES:] = jnp.where(mask, less, zero)

    def pair(lo, count, t):
        here = slice(lo, lo + count)
        rows_t = pl.ds(pl.multiple_of(t * R, R), R) if not isinstance(t, int) else pl.ds(t * R, R)
        kt = qkv_r[1, rows_t, :]
        vat = va[rows_t, :]
        dq = dk = dv = None
        for h in range(per):
            gah = ga[h, here, :]
            e = ex[h, t, here, :]
            ds = (e.astype(F32) * dot_nt(gah, vat)).astype(BF)
            q_term = dot(ds, jnp.where(head_mask(R, h), kt, jnp.zeros((), BF)))
            k_term = dot_tn(ds, qm[h, here, :])
            v_term = dot_tn(e, gah[:, :LANES])
            dq = q_term if dq is None else dq + q_term
            dk = k_term if dk is None else dk + k_term
            dv = v_term if dv is None else dv + v_term
        return dq, dk, dv

    scaled(0, R)
    dq_acc[...] = jnp.zeros((KEYS, LANES), F32)

    @pl.loop(1, NP)
    def _(t):
        dq, dk, dv = pair(0, R, t)
        dq_acc[:R] += dq
        dk_acc[t] = dk
        dv_acc[t] = dv

    part = g_r.at[pl.ds(0, (NP - 1) * R)]
    pltpu.make_async_copy(part, part, gr_sem).wait()
    scaled(R, (NP - 1) * R)
    dk_acc[0] = jnp.zeros((R, LANES), F32)
    dv_acc[0] = jnp.zeros((R, LANES), F32)

    @pl.loop(1, NP + 1)
    def _(i):
        t = lax.rem(i, NP)
        dq, dk, dv = pair(R, (NP - 1) * R, t)
        dq_acc[R:] += dq
        dk = dk_acc[t] + dk
        dv = dv_acc[t] + dv

        @pl.when(i == NP)
        def _():
            dk_acc[0] = dk
            dv_acc[0] = dv

        @pl.when(i < NP)
        def _():
            d_s[1, t] = (dk * from_log2).astype(BF)
            d_s[2, t] = dv.astype(BF)
            for j in (1, 2):
                pltpu.make_async_remote_copy(
                    src_ref=d_s.at[j, t],
                    dst_ref=d_r.at[j, me_p],
                    send_sem=ds_sem,
                    recv_sem=dr_sem.at[j],
                    device_id=(peer(t), me_c),
                    device_id_type=MESH,
                ).start()

    for k in range(1, NP):
        d_s[0, k] = (dq_acc[k * R : (k + 1) * R, :] * scale).astype(BF)
        pltpu.make_async_remote_copy(
            src_ref=d_s.at[0, k],
            dst_ref=d_r.at[0, me_p],
            send_sem=ds_sem,
            recv_sem=dr_sem.at[0],
            device_id=(peer(k), me_c),
            device_id_type=MESH,
        ).start()

    dq, dk, dv = pair(0, R, 0)
    d_r[0, me_p] = ((dq_acc[:R] + dq) * scale).astype(BF)
    d_r[1, me_p] = ((dk_acc[0] + dk) * from_log2).astype(BF)
    d_r[2, me_p] = (dv_acc[0] + dv).astype(BF)

    def landed(j):
        part = d_r.at[j, pl.ds(0, NP - 1)]
        pltpu.make_async_copy(part, part, dr_sem.at[j]).wait()

    landed(1)
    landed(2)
    total = input_term(d_r, w1, 1) + input_term(d_r, w1, 2)
    landed(0)
    total = (total + input_term(d_r, w1, 0)).astype(BF).astype(F32)
    path = norm_grad(x[...].astype(F32), gain1[...], total).astype(BF)
    out[...] = (hil[...] + path.astype(F32)).astype(BF)

    part = qkv_s.at[:, pl.ds(0, NP - 1)]
    pltpu.make_async_copy(part, part, xs_sem).wait()
    part = mix_s.at[pl.ds(0, NP - 1)]
    pltpu.make_async_copy(part, part, ms_sem).wait()
    part = at_s.at[pl.ds(0, (inner - 1) * outer)]
    pltpu.make_async_copy(part, part, cs_sem.at[0]).wait()
    part = at_n.at[pl.ds(0, (outer - 1) * inner)]
    pltpu.make_async_copy(part, part, ns_sem).wait()
    wait_spread(a_s, cs_sem.at[1])
    wait_spread(b_s, cs_sem.at[2])
    part = g_s.at[pl.ds(0, NP - 1)]
    pltpu.make_async_copy(part, part, gs_sem).wait()
    part = d_s.at[:, pl.ds(0, NP - 1)]
    pltpu.make_async_copy(part, part, ds_sem).wait()


def shards(
    points, norm_gain_one, qkv_one, out_one, hilbert_pos,
    norm_gain_two, qkv_two, out_two, hilbert_seg, out_grad,
):
    R, D = points.shape[2], points.shape[3]
    NP, NC = lax.axis_size("patch"), lax.axis_size("curve")
    DEPTH = D // HEADS
    CAP = 2 * R // NC
    KEYS, SLOTS, chunks = NP * R, CAP * NC, D // LANES
    per = LANES // DEPTH
    sub = CAP * chunks
    vmem = pl.BlockSpec(memory_space=pltpu.VMEM)
    hbm = pl.BlockSpec(memory_space=pl.ANY)
    V = pltpu.VMEM
    DMA = pltpu.SemaphoreType.DMA
    scratch = dict(
        x=V((R, D), BF), w1=V((D, 3 * D), BF), o1=V((D, D), BF), w2=V((D, 3 * D), BF),
        o2=V((D, D), BF), og=V((R, D), BF),
        qkv_s=V((3, NP, R, LANES), BF), qkv_r=V((3, KEYS, LANES), BF),
        va=V((KEYS, 2 * LANES), BF), ex=V((per, NP, KEYS, R), BF),
        inv_all=V((KEYS, LANES), F32), mix_all=V((KEYS, LANES), F32),
        mix_s=V((NP, R, LANES), BF), mix_r=V((NP, R, LANES), BF),
        at_s=V((NC, LANES), F32), at_m=V((NC, LANES), F32),
        at_n=V((NC, LANES), F32), at_r=V((NC, LANES), F32),
        tmp=V((NC * sub, LANES), F32),
        a_s=V((NC, sub, LANES), BF), a_r=V((NC, sub, LANES), BF),
        b_s=V((NC, sub, LANES), BF), b_r=V((NC, sub, LANES), BF),
        pk=V((SLOTS, R), BF), gat=V((R, SLOTS), BF), p2=V((R, SLOTS), BF), p2t=V((SLOTS, R), BF),
        bias=V((R, R), F32), hil=V((R, D), F32),
        two=V((3, NP, R, LANES), BF), gtwo=V((NP, R, LANES), BF), dtwo=V((3, NP, R, LANES), BF),
        g_s=V((NP, R, LANES), BF), g_r=V((KEYS, LANES), BF), dq_acc=V((KEYS, LANES), F32),
        d_s=V((3, NP, R, LANES), BF), d_r=V((3, NP, R, LANES), BF),
        qm=V((per, KEYS, LANES), BF), ga=V((per, KEYS, 2 * LANES), BF),
        dk_acc=V((NP, R, LANES), F32), dv_acc=V((NP, R, LANES), F32),
        lsem=DMA((8,)), xs=DMA, xr=DMA((3,)), ms=DMA, mr=DMA, cs=DMA((3,)), cr=DMA((3,)),
        gs=DMA, gr=DMA, ds=DMA, dr=DMA((3,)), ns=DMA, nr=DMA, xq=DMA((NP,)),
    )
    result = pl.pallas_call(
        functools.partial(kernel, NP, NC, R, D, CAP, DEPTH),
        out_shape=jax.ShapeDtypeStruct((R, D), BF),
        in_specs=[hbm] * 6 + [vmem] * 4,
        out_specs=vmem,
        scratch_shapes=list(scratch.values()),
        compiler_params=pltpu.CompilerParams(
            collective_id=0, has_side_effects=True, vmem_limit_bytes=56 * 1024 * 1024
        ),
    )(
        points.reshape(R, D), qkv_one, out_one, qkv_two, out_two, out_grad.reshape(R, D),
        norm_gain_one.reshape(1, D), norm_gain_two.reshape(1, D),
        hilbert_pos.reshape(1, R), hilbert_seg.reshape(1, R),
    )
    return result.reshape(points.shape)


def solution(mesh):
    in_specs = (
        P("curve", "patch", None, None), P(), P(), P(), P("curve", "patch", None),
        P(), P(), P(), P("patch", "curve", None), P("patch", "curve", None, None),
    )
    out_specs = P("curve", "patch", None, None)
    return jax.shard_map(shards, mesh=mesh, in_specs=in_specs, out_specs=out_specs, check_vma=False)
```

```python
import functools
import math

import jax
import jax.numpy as jnp
from jax import lax
from jax.experimental import pallas as pl
from jax.experimental.pallas import tpu as pltpu
from jax.sharding import PartitionSpec as P

HEADS = 16
EPS = 1e-06
F32 = jnp.float32
BF = jnp.bfloat16
MESH = pl.DeviceIdType.MESH
LANES = 128


def dot(a, b):
    return lax.dot_general(a, b, (((1,), (0,)), ((), ())), preferred_element_type=F32)


def dot_nt(a, b):
    return lax.dot_general(a, b, (((1,), (1,)), ((), ())), preferred_element_type=F32)


def dot_tn(a, b):
    return lax.dot_general(a, b, (((0,), (0,)), ((), ())), preferred_element_type=F32)


def iota(shape, dim):
    return lax.broadcasted_iota(jnp.int32, shape, dim)


def norm_scale(rows):
    return lax.rsqrt(jnp.mean(rows * rows, axis=-1, keepdims=True) + EPS)


def norm_grad(rows, gain, cot):
    r = norm_scale(rows)
    c = cot * gain
    inner = jnp.mean(c * rows, axis=-1, keepdims=True)
    return r * (c - rows * (r * r * inner))


def column(row, size):
    eye = iota((size, size), 0) == iota((size, size), 1)
    return jnp.sum(jnp.where(eye, row, 0.0), axis=1, keepdims=True)


def kernel(
    NP, NC, R, D, CAP, DEPTH,
    x_hbm, w1_hbm, o1_hbm, w2_hbm, o2_hbm, og_hbm, gain1, gain2, pos, seg,
    out,
    x, w1, o1, w2, o2, og,
    qkv_s, qkv_r, va, ex, inv_all, mix_all,
    mix_s, mix_r, at_s, at_m, at_n, at_r, tmp, a_s, a_r, b_s, b_r,
    pk, gat, p2, p2t, bias, hil, two, gtwo, dtwo,
    g_s, g_r, dq_acc, d_s, d_r, qm, ga, dk_acc, dv_acc,
    lsem, xs_sem, xr_sem, ms_sem, mr_sem, cs_sem, cr_sem, gs_sem, gr_sem, ds_sem, dr_sem, ns_sem, nr_sem, xq_sem,
):
    me_p = lax.axis_index("patch")
    me_c = lax.axis_index("curve")
    scale = DEPTH ** (-0.5)
    to_log2 = scale * math.log2(math.e)
    from_log2 = math.log(2.0)
    per = LANES // DEPTH
    KEYS = NP * R
    SLOTS = CAP * NC

    thirds = [pl.ds(j * D, D) for j in range(3)]
    moves = [(x_hbm, x)] + [(w1_hbm.at[:, thirds[j]], w1.at[:, thirds[j]]) for j in range(3)]
    moves += [(o1_hbm, o1), (w2_hbm, w2), (o2_hbm, o2), (og_hbm, og)]
    loads = [pltpu.make_async_copy(src, dst, lsem.at[i]) for i, (src, dst) in enumerate(moves)]
    for i in (0, 2, 3, 1):
        loads[i].start()

    barrier = pltpu.get_barrier_semaphore()

    def peer(k):
        return lax.rem(me_p + k, NP)

    inner = 1 << (NC.bit_length() // 2)
    outer = NC // inner
    row, place_in = me_c // inner, lax.rem(me_c, inner)
    greeted = [(peer(k), me_c) for k in range(1, NP)]
    greeted += [(me_p, row * inner + lax.rem(place_in + k, inner)) for k in range(1, inner)]
    greeted += [(me_p, lax.rem(row + k, outer) * inner + place_in) for k in range(1, outer)]
    for device in greeted:
        pl.semaphore_signal(barrier, inc=1, device_id=device, device_id_type=MESH)

    def head_mask(rows, h):
        return iota((rows, LANES), 1) // DEPTH == h

    def far(k):
        return pl.ds((NP - k) % NP * R, R)

    loads[0].wait()
    rows = x[...].astype(F32)
    normed = (rows * norm_scale(rows) * gain1[...]).astype(BF)
    for j in (1, 2, 0):
        loads[1 + j].wait()
        part = dot(normed, w1[:, j * D : (j + 1) * D])
        part = (part * to_log2 if j == 0 else part).astype(BF)
        for p in range(NP):
            qkv_s[j, p] = part[:, p * LANES : (p + 1) * LANES]
        if j == 1:
            pl.semaphore_wait(barrier, len(greeted))
        for k in range(1, NP):
            pltpu.make_async_remote_copy(
                src_ref=qkv_s.at[j, peer(k)],
                dst_ref=qkv_r.at[j, far(k)],
                send_sem=xs_sem,
                recv_sem=xr_sem.at[j] if j else xq_sem.at[NP - k],
                device_id=(peer(k), me_c),
                device_id_type=MESH,
            ).start()
        qkv_r[j, far(0), :] = qkv_s[j, me_p]
    for load in loads[4:]:
        load.start()

    place = pos[...]
    owner_row = (place // R).astype(F32)
    offset_row = (place % R).astype(F32)
    owner_col = column(owner_row, R)
    offset_col = column(offset_row, R)
    same = owner_col == owner_row
    i0, i1 = iota((R, R), 0), iota((R, R), 1)
    rank_row = jnp.sum(jnp.where(same & (i0 < i1), 1.0, 0.0), axis=0, keepdims=True)
    rank_col = jnp.sum(jnp.where(same & (i1 < i0), 1.0, 0.0), axis=1, keepdims=True)
    slot_row = rank_row * NC + owner_row
    slot_col = rank_col * NC + owner_col
    pk[...] = jnp.where(iota((SLOTS, R), 0).astype(F32) == slot_row, 1.0, 0.0).astype(BF)
    gat[...] = jnp.where(iota((R, SLOTS), 1).astype(F32) == slot_col, 1.0, 0.0).astype(BF)
    table = dot(pk[...], jnp.broadcast_to(offset_col + 1.0, (R, LANES)).astype(BF))
    lane = iota((NC, LANES), 1)
    note = jnp.zeros((NC, LANES), F32)
    for r in range(CAP):
        note = jnp.where(lane == r, table[r * NC : (r + 1) * NC], note)
    for z in range(outer):
        at_s[pl.ds(z, inner, outer), :] = note[z * inner : (z + 1) * inner]

    def line(k, count, at):
        return pl.ds(pl.multiple_of(lax.rem(at + k, count) * (NC // count), NC // count), NC // count)

    for k in range(1, inner):
        pltpu.make_async_remote_copy(
            src_ref=at_s.at[line(k, inner, place_in)],
            dst_ref=at_m.at[line(0, inner, place_in)],
            send_sem=cs_sem.at[0],
            recv_sem=cr_sem.at[0],
            device_id=(me_p, row * inner + lax.rem(place_in + k, inner)),
            device_id_type=MESH,
        ).start()
    at_m[line(0, inner, place_in), :] = at_s[line(0, inner, place_in), :]

    def spread(src, dst, send_sem, recv_sem):
        @pl.loop(1, NC)
        def _(k):
            other = lax.rem(me_c + lax.rem(k * 51, NC), NC)
            pltpu.make_async_remote_copy(
                src_ref=src.at[other],
                dst_ref=dst.at[me_c],
                send_sem=send_sem,
                recv_sem=recv_sem,
                device_id=(me_p, other),
                device_id_type=MESH,
            ).start()

        dst[me_c] = src[me_c]

    def wait_spread(buf, sem):
        part = buf.at[pl.ds(0, NC - 1)]
        pltpu.make_async_copy(part, part, sem).wait()

    loads[6].wait()
    loads[7].wait()
    g2 = dot_nt(og[...], o2[...]).astype(BF)
    for g in range(NP):
        gtwo[g] = g2[:, g * LANES : (g + 1) * LANES]
    seg_row = seg[...].astype(F32)
    bias[...] = jnp.where(column(seg_row, R) == seg_row, 0.0, -1e30)
    part = at_m.at[pl.ds(0, (inner - 1) * outer)]
    pltpu.make_async_copy(part, part, cr_sem.at[0]).wait()
    for z in range(outer):
        at_n[z * inner : (z + 1) * inner, :] = at_m[pl.ds(z, inner, outer), :]
    for k in range(1, outer):
        pltpu.make_async_remote_copy(
            src_ref=at_n.at[line(k, outer, row)],
            dst_ref=at_r.at[line(0, outer, row)],
            send_sem=ns_sem,
            recv_sem=nr_sem,
            device_id=(me_p, lax.rem(row + k, outer) * inner + place_in),
            device_id_type=MESH,
        ).start()
    at_r[line(0, outer, row), :] = at_n[line(0, outer, row), :]

    def arrive(j):
        part = qkv_r.at[j, pl.ds(0, (NP - 1) * R)]
        pltpu.make_async_copy(part, part, xr_sem.at[j]).wait()

    arrive(1)
    arrive(2)
    va[:, :LANES] = qkv_r[2]
    va[:, LANES:] = jnp.ones((KEYS, LANES), BF)

    for s in range(NP):
        rows_s = pl.ds(s * R, R)

        if s > 0:
            part = qkv_r.at[0, rows_s]
            pltpu.make_async_copy(part, part, xq_sem.at[s]).wait()

        qs = qkv_r[0, rows_s, :]
        keys = qkv_r[1]
        mixed = jnp.zeros((R, LANES), F32)
        inv = jnp.zeros((R, LANES), F32)
        for h in range(per):
            mask = head_mask(R, h)
            qh = jnp.where(mask, qs, jnp.zeros((), BF))
            qm[h, rows_s, :] = qh
            scores = dot_nt(qh, keys)
            top = jnp.max(scores, axis=1, keepdims=True)
            e = jnp.exp2(scores - top).astype(BF)
            for t in range(NP):
                ex[h, t, rows_s, :] = e[:, t * R : (t + 1) * R]
            both = dot(e, va[...])
            one = 1.0 / both[:, LANES:]
            mixed = jnp.where(mask, both[:, :LANES] * one, mixed)
            inv = jnp.where(mask, one, inv)
        mix_all[rows_s, :] = mixed
        inv_all[rows_s, :] = inv
        mix_s[s] = mixed.astype(BF)

        if s > 0:
            pltpu.make_async_remote_copy(
                src_ref=mix_s.at[s],
                dst_ref=mix_r.at[me_p],
                send_sem=ms_sem,
                recv_sem=mr_sem,
                device_id=(peer(s), me_c),
                device_id_type=MESH,
            ).start()

    mix_r[me_p] = mix_s[0]

    part = mix_r.at[pl.ds(0, NP - 1)]
    pltpu.make_async_copy(part, part, mr_sem).wait()
    loads[4].wait()
    mixed = jnp.concatenate([mix_r[p] for p in range(NP)], axis=1)
    moved = (x[...].astype(F32) + dot(mixed, o1[...])).astype(BF)

    chunks = D // LANES
    sub = CAP * chunks

    def pack(choose, what, dst):
        y = dot(choose, what)
        for r in range(CAP):
            for c in range(chunks):
                tmp[pl.ds(c * CAP + r, NC, sub), :] = y[
                    r * NC : (r + 1) * NC, c * LANES : (c + 1) * LANES
                ]
        dst[...] = tmp[...].reshape(NC, sub, LANES).astype(BF)

    def unpack(choose, src):
        tmp[...] = src[...].astype(F32).reshape(NC * sub, LANES)
        got = jnp.concatenate(
            [
                jnp.concatenate([tmp[pl.ds(c * CAP + r, NC, sub), :] for c in range(chunks)], axis=1)
                for r in range(CAP)
            ],
            axis=0,
        ).astype(BF)
        return dot(choose, got)

    pack(pk[...], moved, a_s)
    part = at_r.at[pl.ds(0, (outer - 1) * inner)]
    pltpu.make_async_copy(part, part, nr_sem).wait()
    spread(a_s, a_r, cs_sem.at[1], cr_sem.at[1])

    landing = at_r[...]
    turned = landing.T
    for r in range(CAP):
        p2[:, r * NC : (r + 1) * NC] = jnp.where(
            (iota((R, NC), 0) + 1).astype(F32) == turned[r : r + 1, :], 1.0, 0.0
        ).astype(BF)
        p2t[r * NC : (r + 1) * NC, :] = jnp.where(
            (iota((NC, R), 1) + 1).astype(F32) == landing[:, r : r + 1], 1.0, 0.0
        ).astype(BF)

    loads[5].wait()
    wait_spread(a_r, cr_sem.at[1])

    hil[...] = unpack(p2[...], a_r)
    rows = hil[...]
    normed = (rows * norm_scale(rows) * gain2[...]).astype(BF)
    for j in range(3):
        part = dot(normed, w2[:, j * D : (j + 1) * D])
        part = (part * to_log2 if j == 0 else part).astype(BF)
        for g in range(NP):
            two[j, g] = part[:, g * LANES : (g + 1) * LANES]

    def stack(m):
        zero = jnp.zeros((), m.dtype)
        return jnp.concatenate([jnp.where(head_mask(R, h), m, zero) for h in range(per)], axis=0)

    for g in range(NP):
        qg, kg, vg = stack(two[0, g]), two[1, g], two[2, g]
        va2 = jnp.concatenate([vg, jnp.ones((R, LANES), BF)], axis=1)
        scores = dot_nt(qg, kg) + jnp.concatenate([bias[...]] * per, axis=0)
        e = jnp.exp2(scores - jnp.max(scores, axis=1, keepdims=True)).astype(BF)
        both = dot(e, va2)
        one = 1.0 / both[:, LANES:]
        gi = stack(gtwo[g].astype(F32)) * one
        less = -gi * (both[:, :LANES] * one)
        gib = gi.astype(BF)
        lhs = jnp.concatenate([gib, less.astype(BF)], axis=1)
        ds = (e.astype(F32) * dot_nt(lhs, va2)).astype(BF)
        full = dot(ds, kg)
        dq = full[:R]
        for h in range(1, per):
            dq = jnp.where(head_mask(R, h), full[h * R : (h + 1) * R], dq)
        dtwo[0, g] = (dq * scale).astype(BF)
        dtwo[1, g] = (dot_tn(ds, qg) * from_log2).astype(BF)
        dtwo[2, g] = dot_tn(e, gib).astype(BF)

    def input_term(d, w, j):
        piece = jnp.concatenate([d[j, g] for g in range(NP)], axis=1)
        return dot_nt(piece, w[:, j * D : (j + 1) * D])

    def input_grad(d, w):
        total = input_term(d, w, 0) + input_term(d, w, 1) + input_term(d, w, 2)
        return total.astype(BF).astype(F32)

    path = norm_grad(hil[...], gain2[...], input_grad(dtwo, w2)).astype(BF)
    hil_grad = (og[...].astype(F32) + path.astype(F32)).astype(BF)

    pack(p2t[...], hil_grad, b_s)
    spread(b_s, b_r, cs_sem.at[2], cr_sem.at[2])
    wait_spread(b_r, cr_sem.at[2])
    moved_grad = unpack(gat[...], b_r).astype(BF)
    hil[...] = moved_grad.astype(F32)

    g1 = dot_nt(moved_grad, o1[...]).astype(BF)
    for p in range(NP):
        g_s[p] = g1[:, p * LANES : (p + 1) * LANES]
    for k in range(1, NP):
        pltpu.make_async_remote_copy(
            src_ref=g_s.at[peer(k)],
            dst_ref=g_r.at[far(k)],
            send_sem=gs_sem,
            recv_sem=gr_sem,
            device_id=(peer(k), me_c),
            device_id_type=MESH,
        ).start()
    g_r[far(0), :] = g_s[me_p]

    def scaled(lo, count):
        here = slice(lo, lo + count)
        gi = g_r[here, :].astype(F32) * inv_all[here, :]
        less = (-gi * mix_all[here, :]).astype(BF)
        gi = gi.astype(BF)
        zero = jnp.zeros((), BF)
        for h in range(per):
            mask = head_mask(count, h)
            ga[h, here, :LANES] = jnp.where(mask, gi, zero)
            ga[h, here, LANES:] = jnp.where(mask, less, zero)

    def pair(lo, count, t):
        here = slice(lo, lo + count)
        rows_t = pl.ds(t * R, R)
        kt = qkv_r[1, rows_t, :]
        vat = va[rows_t, :]
        dq = dk = dv = None
        for h in range(per):
            gah = ga[h, here, :]
            e = ex[h, t, here, :]
            ds = (e.astype(F32) * dot_nt(gah, vat)).astype(BF)
            q_term = dot(ds, jnp.where(head_mask(R, h), kt, jnp.zeros((), BF)))
            k_term = dot_tn(ds, qm[h, here, :])
            v_term = dot_tn(e, gah[:, :LANES])
            dq = q_term if dq is None else dq + q_term
            dk = k_term if dk is None else dk + k_term
            dv = v_term if dv is None else dv + v_term
        return dq, dk, dv

    scaled(0, R)
    dq_acc[...] = jnp.zeros((KEYS, LANES), F32)

    for t in range(1, NP):
        dq, dk, dv = pair(0, R, t)
        dq_acc[:R] += dq
        dk_acc[t] = dk
        dv_acc[t] = dv

    part = g_r.at[pl.ds(0, (NP - 1) * R)]
    pltpu.make_async_copy(part, part, gr_sem).wait()
    scaled(R, (NP - 1) * R)
    dk_acc[0] = jnp.zeros((R, LANES), F32)
    dv_acc[0] = jnp.zeros((R, LANES), F32)

    for t in (*range(1, NP), 0):
        dq, dk, dv = pair(R, (NP - 1) * R, t)
        dq_acc[R:] += dq
        dk = dk_acc[t] + dk
        dv = dv_acc[t] + dv

        if t == 0:
            dk_acc[0] = dk
            dv_acc[0] = dv
        else:
            d_s[1, t] = (dk * from_log2).astype(BF)
            d_s[2, t] = dv.astype(BF)
            for j in (1, 2):
                pltpu.make_async_remote_copy(
                    src_ref=d_s.at[j, t],
                    dst_ref=d_r.at[j, me_p],
                    send_sem=ds_sem,
                    recv_sem=dr_sem.at[j],
                    device_id=(peer(t), me_c),
                    device_id_type=MESH,
                ).start()

    for k in range(1, NP):
        d_s[0, k] = (dq_acc[k * R : (k + 1) * R, :] * scale).astype(BF)
        pltpu.make_async_remote_copy(
            src_ref=d_s.at[0, k],
            dst_ref=d_r.at[0, me_p],
            send_sem=ds_sem,
            recv_sem=dr_sem.at[0],
            device_id=(peer(k), me_c),
            device_id_type=MESH,
        ).start()

    dq, dk, dv = pair(0, R, 0)
    d_r[0, me_p] = ((dq_acc[:R] + dq) * scale).astype(BF)
    d_r[1, me_p] = ((dk_acc[0] + dk) * from_log2).astype(BF)
    d_r[2, me_p] = (dv_acc[0] + dv).astype(BF)

    def landed(j):
        part = d_r.at[j, pl.ds(0, NP - 1)]
        pltpu.make_async_copy(part, part, dr_sem.at[j]).wait()

    landed(1)
    landed(2)
    total = input_term(d_r, w1, 1) + input_term(d_r, w1, 2)
    landed(0)
    total = (total + input_term(d_r, w1, 0)).astype(BF).astype(F32)
    path = norm_grad(x[...].astype(F32), gain1[...], total).astype(BF)
    out[...] = (hil[...] + path.astype(F32)).astype(BF)

    part = qkv_s.at[:, pl.ds(0, NP - 1)]
    pltpu.make_async_copy(part, part, xs_sem).wait()
    part = mix_s.at[pl.ds(0, NP - 1)]
    pltpu.make_async_copy(part, part, ms_sem).wait()
    part = at_s.at[pl.ds(0, (inner - 1) * outer)]
    pltpu.make_async_copy(part, part, cs_sem.at[0]).wait()
    part = at_n.at[pl.ds(0, (outer - 1) * inner)]
    pltpu.make_async_copy(part, part, ns_sem).wait()
    wait_spread(a_s, cs_sem.at[1])
    wait_spread(b_s, cs_sem.at[2])
    part = g_s.at[pl.ds(0, NP - 1)]
    pltpu.make_async_copy(part, part, gs_sem).wait()
    part = d_s.at[:, pl.ds(0, NP - 1)]
    pltpu.make_async_copy(part, part, ds_sem).wait()


def shards(
    points, norm_gain_one, qkv_one, out_one, hilbert_pos,
    norm_gain_two, qkv_two, out_two, hilbert_seg, out_grad,
):
    R, D = points.shape[2], points.shape[3]
    NP, NC = lax.axis_size("patch"), lax.axis_size("curve")
    DEPTH = D // HEADS
    CAP = 2 * R // NC
    KEYS, SLOTS, chunks = NP * R, CAP * NC, D // LANES
    per = LANES // DEPTH
    sub = CAP * chunks
    vmem = pl.BlockSpec(memory_space=pltpu.VMEM)
    hbm = pl.BlockSpec(memory_space=pl.ANY)
    V = pltpu.VMEM
    DMA = pltpu.SemaphoreType.DMA
    scratch = dict(
        x=V((R, D), BF), w1=V((D, 3 * D), BF), o1=V((D, D), BF), w2=V((D, 3 * D), BF),
        o2=V((D, D), BF), og=V((R, D), BF),
        qkv_s=V((3, NP, R, LANES), BF), qkv_r=V((3, KEYS, LANES), BF),
        va=V((KEYS, 2 * LANES), BF), ex=V((per, NP, KEYS, R), BF),
        inv_all=V((KEYS, LANES), F32), mix_all=V((KEYS, LANES), F32),
        mix_s=V((NP, R, LANES), BF), mix_r=V((NP, R, LANES), BF),
        at_s=V((NC, LANES), F32), at_m=V((NC, LANES), F32),
        at_n=V((NC, LANES), F32), at_r=V((NC, LANES), F32),
        tmp=V((NC * sub, LANES), F32),
        a_s=V((NC, sub, LANES), BF), a_r=V((NC, sub, LANES), BF),
        b_s=V((NC, sub, LANES), BF), b_r=V((NC, sub, LANES), BF),
        pk=V((SLOTS, R), BF), gat=V((R, SLOTS), BF), p2=V((R, SLOTS), BF), p2t=V((SLOTS, R), BF),
        bias=V((R, R), F32), hil=V((R, D), F32),
        two=V((3, NP, R, LANES), BF), gtwo=V((NP, R, LANES), BF), dtwo=V((3, NP, R, LANES), BF),
        g_s=V((NP, R, LANES), BF), g_r=V((KEYS, LANES), BF), dq_acc=V((KEYS, LANES), F32),
        d_s=V((3, NP, R, LANES), BF), d_r=V((3, NP, R, LANES), BF),
        qm=V((per, KEYS, LANES), BF), ga=V((per, KEYS, 2 * LANES), BF),
        dk_acc=V((NP, R, LANES), F32), dv_acc=V((NP, R, LANES), F32),
        lsem=DMA((8,)), xs=DMA, xr=DMA((3,)), ms=DMA, mr=DMA, cs=DMA((3,)), cr=DMA((3,)),
        gs=DMA, gr=DMA, ds=DMA, dr=DMA((3,)), ns=DMA, nr=DMA, xq=DMA((NP,)),
    )
    result = pl.pallas_call(
        functools.partial(kernel, NP, NC, R, D, CAP, DEPTH),
        out_shape=jax.ShapeDtypeStruct((R, D), BF),
        in_specs=[hbm] * 6 + [vmem] * 4,
        out_specs=vmem,
        scratch_shapes=list(scratch.values()),
        compiler_params=pltpu.CompilerParams(
            collective_id=0, has_side_effects=True, vmem_limit_bytes=56 * 1024 * 1024
        ),
    )(
        points.reshape(R, D), qkv_one, out_one, qkv_two, out_two, out_grad.reshape(R, D),
        norm_gain_one.reshape(1, D), norm_gain_two.reshape(1, D),
        hilbert_pos.reshape(1, R), hilbert_seg.reshape(1, R),
    )
    return result.reshape(points.shape)


def solution(mesh):
    in_specs = (
        P("curve", "patch", None, None), P(), P(), P(), P("curve", "patch", None),
        P(), P(), P(), P("patch", "curve", None), P("patch", "curve", None, None),
    )
    out_specs = P("curve", "patch", None, None)
    return jax.shard_map(shards, mesh=mesh, in_specs=in_specs, out_specs=out_specs, check_vma=False)
```

```python
import functools
import math

import jax
import jax.numpy as jnp
from jax import lax
from jax.experimental import pallas as pl
from jax.experimental.pallas import tpu as pltpu
from jax.sharding import PartitionSpec as P

HEADS = 16
EPS = 1e-06
F32 = jnp.float32
BF = jnp.bfloat16
MESH = pl.DeviceIdType.MESH
LANES = 128


def dot(a, b):
    return lax.dot_general(a, b, (((1,), (0,)), ((), ())), preferred_element_type=F32)


def dot_nt(a, b):
    return lax.dot_general(a, b, (((1,), (1,)), ((), ())), preferred_element_type=F32)


def dot_tn(a, b):
    return lax.dot_general(a, b, (((0,), (0,)), ((), ())), preferred_element_type=F32)


def iota(shape, dim):
    return lax.broadcasted_iota(jnp.int32, shape, dim)


def norm_scale(rows):
    return lax.rsqrt(jnp.mean(rows * rows, axis=-1, keepdims=True) + EPS)


def norm_grad(rows, gain, cot):
    r = norm_scale(rows)
    c = cot * gain
    inner = jnp.mean(c * rows, axis=-1, keepdims=True)
    return r * (c - rows * (r * r * inner))


def column(row, size):
    eye = iota((size, size), 0) == iota((size, size), 1)
    return jnp.sum(jnp.where(eye, row, 0.0), axis=1, keepdims=True)


def kernel(
    NP, NC, R, D, CAP, DEPTH,
    x_hbm, w1_hbm, o1_hbm, w2_hbm, o2_hbm, og_hbm, gain1, gain2, pos, seg,
    out,
    x, w1, o1, w2, o2, og,
    qkv_s, qkv_r, va, ex, inv_all, mix_all,
    mix_s, mix_r, at_s, at_m, at_n, at_r, tmp, a_s, a_r, b_s, b_r,
    pk, gat, p2, p2t, bias, hil, two, gtwo, dtwo,
    g_s, g_r, dq_acc, d_s, d_r, qm, ga, dk_acc, dv_acc,
    lsem, xs_sem, xr_sem, ms_sem, mr_sem, cs_sem, cr_sem, gs_sem, gr_sem, ds_sem, dr_sem, ns_sem, nr_sem, xq_sem,
):
    me_p = lax.axis_index("patch")
    me_c = lax.axis_index("curve")
    scale = DEPTH ** (-0.5)
    to_log2 = scale * math.log2(math.e)
    from_log2 = math.log(2.0)
    per = LANES // DEPTH
    KEYS = NP * R
    SLOTS = CAP * NC

    thirds = [pl.ds(j * D, D) for j in range(3)]
    moves = [(x_hbm, x)] + [(w1_hbm.at[:, thirds[j]], w1.at[:, thirds[j]]) for j in range(3)]
    moves += [(o1_hbm, o1), (w2_hbm, w2), (o2_hbm, o2), (og_hbm, og)]
    loads = [pltpu.make_async_copy(src, dst, lsem.at[i]) for i, (src, dst) in enumerate(moves)]
    for i in (0, 2, 3, 1):
        loads[i].start()

    barrier = pltpu.get_barrier_semaphore()

    def peer(k):
        return lax.rem(me_p + k, NP)

    inner = 1 << (NC.bit_length() // 2)
    outer = NC // inner
    row, place_in = me_c // inner, lax.rem(me_c, inner)
    greeted = [(peer(k), me_c) for k in range(1, NP)]
    greeted += [(me_p, row * inner + lax.rem(place_in + k, inner)) for k in range(1, inner)]
    greeted += [(me_p, lax.rem(row + k, outer) * inner + place_in) for k in range(1, outer)]
    for device in greeted:
        pl.semaphore_signal(barrier, inc=1, device_id=device, device_id_type=MESH)

    def head_mask(rows, h):
        return iota((rows, LANES), 1) // DEPTH == h

    def far(k):
        return pl.ds((NP - k) % NP * R, R)

    loads[0].wait()
    rows = x[...].astype(F32)
    normed = (rows * norm_scale(rows) * gain1[...]).astype(BF)
    for j in (1, 2, 0):
        loads[1 + j].wait()
        part = dot(normed, w1[:, j * D : (j + 1) * D])
        part = (part * to_log2 if j == 0 else part).astype(BF)
        for p in range(NP):
            qkv_s[j, p] = part[:, p * LANES : (p + 1) * LANES]
        if j == 1:
            pl.semaphore_wait(barrier, len(greeted))
        for k in range(1, NP):
            pltpu.make_async_remote_copy(
                src_ref=qkv_s.at[j, peer(k)],
                dst_ref=qkv_r.at[j, far(k)],
                send_sem=xs_sem,
                recv_sem=xr_sem.at[j] if j else xq_sem.at[NP - k],
                device_id=(peer(k), me_c),
                device_id_type=MESH,
            ).start()
        qkv_r[j, far(0), :] = qkv_s[j, me_p]
    for load in loads[4:]:
        load.start()

    place = pos[...]
    owner_row = (place // R).astype(F32)
    offset_row = (place % R).astype(F32)
    owner_col = column(owner_row, R)
    offset_col = column(offset_row, R)
    same = owner_col == owner_row
    i0, i1 = iota((R, R), 0), iota((R, R), 1)
    rank_row = jnp.sum(jnp.where(same & (i0 < i1), 1.0, 0.0), axis=0, keepdims=True)
    rank_col = jnp.sum(jnp.where(same & (i1 < i0), 1.0, 0.0), axis=1, keepdims=True)
    slot_row = rank_row * NC + owner_row
    slot_col = rank_col * NC + owner_col
    pk[...] = jnp.where(iota((SLOTS, R), 0).astype(F32) == slot_row, 1.0, 0.0).astype(BF)
    gat[...] = jnp.where(iota((R, SLOTS), 1).astype(F32) == slot_col, 1.0, 0.0).astype(BF)
    table = dot(pk[...], jnp.broadcast_to(offset_col + 1.0, (R, LANES)).astype(BF))
    lane = iota((NC, LANES), 1)
    note = jnp.zeros((NC, LANES), F32)
    for r in range(CAP):
        note = jnp.where(lane == r, table[r * NC : (r + 1) * NC], note)
    for z in range(outer):
        at_s[pl.ds(z, inner, outer), :] = note[z * inner : (z + 1) * inner]

    def line(k, count, at):
        return pl.ds(pl.multiple_of(lax.rem(at + k, count) * (NC // count), NC // count), NC // count)

    for k in range(1, inner):
        pltpu.make_async_remote_copy(
            src_ref=at_s.at[line(k, inner, place_in)],
            dst_ref=at_m.at[line(0, inner, place_in)],
            send_sem=cs_sem.at[0],
            recv_sem=cr_sem.at[0],
            device_id=(me_p, row * inner + lax.rem(place_in + k, inner)),
            device_id_type=MESH,
        ).start()
    at_m[line(0, inner, place_in), :] = at_s[line(0, inner, place_in), :]

    def spread(src, dst, send_sem, recv_sem):
        @pl.loop(1, NC)
        def _(k):
            turn = lax.rem(k * 37, NC)
            there = lax.rem(row + turn // inner, outer) * inner
            chip = lax.rem(place_in // 2 + lax.rem(turn, inner) // 2, inner // 2) * 2
            other = there + chip + lax.rem(place_in + turn, 2)
            pltpu.make_async_remote_copy(
                src_ref=src.at[other],
                dst_ref=dst.at[me_c],
                send_sem=send_sem,
                recv_sem=recv_sem,
                device_id=(me_p, other),
                device_id_type=MESH,
            ).start()

        dst[me_c] = src[me_c]

    def wait_spread(buf, sem):
        part = buf.at[pl.ds(0, NC - 1)]
        pltpu.make_async_copy(part, part, sem).wait()

    loads[6].wait()
    loads[7].wait()
    g2 = dot_nt(og[...], o2[...]).astype(BF)
    for g in range(NP):
        gtwo[g] = g2[:, g * LANES : (g + 1) * LANES]
    seg_row = seg[...].astype(F32)
    bias[...] = jnp.where(column(seg_row, R) == seg_row, 0.0, -1e30)
    part = at_m.at[pl.ds(0, (inner - 1) * outer)]
    pltpu.make_async_copy(part, part, cr_sem.at[0]).wait()
    for z in range(outer):
        at_n[z * inner : (z + 1) * inner, :] = at_m[pl.ds(z, inner, outer), :]
    for k in range(1, outer):
        pltpu.make_async_remote_copy(
            src_ref=at_n.at[line(k, outer, row)],
            dst_ref=at_r.at[line(0, outer, row)],
            send_sem=ns_sem,
            recv_sem=nr_sem,
            device_id=(me_p, lax.rem(row + k, outer) * inner + place_in),
            device_id_type=MESH,
        ).start()
    at_r[line(0, outer, row), :] = at_n[line(0, outer, row), :]

    def arrive(j):
        part = qkv_r.at[j, pl.ds(0, (NP - 1) * R)]
        pltpu.make_async_copy(part, part, xr_sem.at[j]).wait()

    arrive(1)
    arrive(2)
    va[:, :LANES] = qkv_r[2]
    va[:, LANES:] = jnp.ones((KEYS, LANES), BF)

    @pl.loop(0, NP)
    def _(s):
        rows_s = pl.ds(pl.multiple_of(s * R, R), R)

        @pl.when(s > 0)
        def _():
            part = qkv_r.at[0, rows_s]
            pltpu.make_async_copy(part, part, xq_sem.at[s]).wait()

        qs = qkv_r[0, rows_s, :]
        keys = qkv_r[1]
        mixed = jnp.zeros((R, LANES), F32)
        inv = jnp.zeros((R, LANES), F32)
        for h in range(per):
            mask = head_mask(R, h)
            qh = jnp.where(mask, qs, jnp.zeros((), BF))
            qm[h, rows_s, :] = qh
            scores = dot_nt(qh, keys)
            top = jnp.max(scores, axis=1, keepdims=True)
            e = jnp.exp2(scores - top).astype(BF)
            for t in range(NP):
                ex[h, t, rows_s, :] = e[:, t * R : (t + 1) * R]
            both = dot(e, va[...])
            one = 1.0 / both[:, LANES:]
            mixed = jnp.where(mask, both[:, :LANES] * one, mixed)
            inv = jnp.where(mask, one, inv)
        mix_all[rows_s, :] = mixed
        inv_all[rows_s, :] = inv
        mix_s[s] = mixed.astype(BF)

        @pl.when(s > 0)
        def _():
            pltpu.make_async_remote_copy(
                src_ref=mix_s.at[s],
                dst_ref=mix_r.at[me_p],
                send_sem=ms_sem,
                recv_sem=mr_sem,
                device_id=(peer(s), me_c),
                device_id_type=MESH,
            ).start()

    mix_r[me_p] = mix_s[0]

    part = mix_r.at[pl.ds(0, NP - 1)]
    pltpu.make_async_copy(part, part, mr_sem).wait()
    loads[4].wait()
    mixed = jnp.concatenate([mix_r[p] for p in range(NP)], axis=1)
    moved = (x[...].astype(F32) + dot(mixed, o1[...])).astype(BF)

    chunks = D // LANES
    sub = CAP * chunks

    def pack(choose, what, dst):
        y = dot(choose, what)
        for r in range(CAP):
            for c in range(chunks):
                tmp[pl.ds(c * CAP + r, NC, sub), :] = y[
                    r * NC : (r + 1) * NC, c * LANES : (c + 1) * LANES
                ]
        dst[...] = tmp[...].reshape(NC, sub, LANES).astype(BF)

    def unpack(choose, src):
        tmp[...] = src[...].astype(F32).reshape(NC * sub, LANES)
        got = jnp.concatenate(
            [
                jnp.concatenate([tmp[pl.ds(c * CAP + r, NC, sub), :] for c in range(chunks)], axis=1)
                for r in range(CAP)
            ],
            axis=0,
        ).astype(BF)
        return dot(choose, got)

    pack(pk[...], moved, a_s)
    part = at_r.at[pl.ds(0, (outer - 1) * inner)]
    pltpu.make_async_copy(part, part, nr_sem).wait()
    spread(a_s, a_r, cs_sem.at[1], cr_sem.at[1])

    landing = at_r[...]
    turned = landing.T
    for r in range(CAP):
        p2[:, r * NC : (r + 1) * NC] = jnp.where(
            (iota((R, NC), 0) + 1).astype(F32) == turned[r : r + 1, :], 1.0, 0.0
        ).astype(BF)
        p2t[r * NC : (r + 1) * NC, :] = jnp.where(
            (iota((NC, R), 1) + 1).astype(F32) == landing[:, r : r + 1], 1.0, 0.0
        ).astype(BF)

    loads[5].wait()
    wait_spread(a_r, cr_sem.at[1])

    hil[...] = unpack(p2[...], a_r)
    rows = hil[...]
    normed = (rows * norm_scale(rows) * gain2[...]).astype(BF)
    for j in range(3):
        part = dot(normed, w2[:, j * D : (j + 1) * D])
        part = (part * to_log2 if j == 0 else part).astype(BF)
        for g in range(NP):
            two[j, g] = part[:, g * LANES : (g + 1) * LANES]

    def stack(m):
        zero = jnp.zeros((), m.dtype)
        return jnp.concatenate([jnp.where(head_mask(R, h), m, zero) for h in range(per)], axis=0)

    for g in range(NP):
        qg, kg, vg = stack(two[0, g]), two[1, g], two[2, g]
        va2 = jnp.concatenate([vg, jnp.ones((R, LANES), BF)], axis=1)
        scores = dot_nt(qg, kg) + jnp.concatenate([bias[...]] * per, axis=0)
        e = jnp.exp2(scores - jnp.max(scores, axis=1, keepdims=True)).astype(BF)
        both = dot(e, va2)
        one = 1.0 / both[:, LANES:]
        gi = stack(gtwo[g].astype(F32)) * one
        less = -gi * (both[:, :LANES] * one)
        gib = gi.astype(BF)
        lhs = jnp.concatenate([gib, less.astype(BF)], axis=1)
        ds = (e.astype(F32) * dot_nt(lhs, va2)).astype(BF)
        full = dot(ds, kg)
        dq = full[:R]
        for h in range(1, per):
            dq = jnp.where(head_mask(R, h), full[h * R : (h + 1) * R], dq)
        dtwo[0, g] = (dq * scale).astype(BF)
        dtwo[1, g] = (dot_tn(ds, qg) * from_log2).astype(BF)
        dtwo[2, g] = dot_tn(e, gib).astype(BF)

    def input_term(d, w, j):
        piece = jnp.concatenate([d[j, g] for g in range(NP)], axis=1)
        return dot_nt(piece, w[:, j * D : (j + 1) * D])

    def input_grad(d, w):
        total = input_term(d, w, 0) + input_term(d, w, 1) + input_term(d, w, 2)
        return total.astype(BF).astype(F32)

    path = norm_grad(hil[...], gain2[...], input_grad(dtwo, w2)).astype(BF)
    hil_grad = (og[...].astype(F32) + path.astype(F32)).astype(BF)

    pack(p2t[...], hil_grad, b_s)
    spread(b_s, b_r, cs_sem.at[2], cr_sem.at[2])
    wait_spread(b_r, cr_sem.at[2])
    moved_grad = unpack(gat[...], b_r).astype(BF)
    hil[...] = moved_grad.astype(F32)

    g1 = dot_nt(moved_grad, o1[...]).astype(BF)
    for p in range(NP):
        g_s[p] = g1[:, p * LANES : (p + 1) * LANES]
    for k in range(1, NP):
        pltpu.make_async_remote_copy(
            src_ref=g_s.at[peer(k)],
            dst_ref=g_r.at[far(k)],
            send_sem=gs_sem,
            recv_sem=gr_sem.at[NP - k],
            device_id=(peer(k), me_c),
            device_id_type=MESH,
        ).start()
    g_r[far(0), :] = g_s[me_p]

    def scaled(lo, count):
        here = slice(lo, lo + count)
        gi = g_r[here, :].astype(F32) * inv_all[here, :]
        less = (-gi * mix_all[here, :]).astype(BF)
        gi = gi.astype(BF)
        zero = jnp.zeros((), BF)
        for h in range(per):
            mask = head_mask(count, h)
            ga[h, here, :LANES] = jnp.where(mask, gi, zero)
            ga[h, here, LANES:] = jnp.where(mask, less, zero)

    def pair(lo, count, t):
        here = slice(lo, lo + count)
        rows_t = pl.ds(pl.multiple_of(t * R, R), R) if not isinstance(t, int) else pl.ds(t * R, R)
        kt = qkv_r[1, rows_t, :]
        vat = va[rows_t, :]
        dq = dk = dv = None
        for h in range(per):
            gah = ga[h, here, :]
            e = ex[h, t, here, :]
            ds = (e.astype(F32) * dot_nt(gah, vat)).astype(BF)
            q_term = dot(ds, jnp.where(head_mask(R, h), kt, jnp.zeros((), BF)))
            k_term = dot_tn(ds, qm[h, here, :])
            v_term = dot_tn(e, gah[:, :LANES])
            dq = q_term if dq is None else dq + q_term
            dk = k_term if dk is None else dk + k_term
            dv = v_term if dv is None else dv + v_term
        return dq, dk, dv

    scaled(0, R)
    dq_acc[...] = jnp.zeros((KEYS, LANES), F32)

    @pl.loop(1, NP)
    def _(t):
        dq, dk, dv = pair(0, R, t)
        dq_acc[:R] += dq
        dk_acc[t] = dk
        dv_acc[t] = dv

    for k in (1, *range(NP - 1, 1, -1)):
        part = g_r.at[pl.ds(k * R, R)]
        pltpu.make_async_copy(part, part, gr_sem.at[k]).wait()
        scaled(k * R, R)
    dk_acc[0] = jnp.zeros((R, LANES), F32)
    dv_acc[0] = jnp.zeros((R, LANES), F32)

    @pl.loop(1, NP + 1)
    def _(i):
        t = lax.rem(i, NP)
        dq, dk, dv = pair(R, (NP - 1) * R, t)
        dq_acc[R:] += dq
        dk = dk_acc[t] + dk
        dv = dv_acc[t] + dv

        @pl.when(i == NP)
        def _():
            dk_acc[0] = dk
            dv_acc[0] = dv

        @pl.when(i < NP)
        def _():
            d_s[1, t] = (dk * from_log2).astype(BF)
            d_s[2, t] = dv.astype(BF)
            for j in (1, 2):
                pltpu.make_async_remote_copy(
                    src_ref=d_s.at[j, t],
                    dst_ref=d_r.at[j, me_p],
                    send_sem=ds_sem,
                    recv_sem=dr_sem.at[j],
                    device_id=(peer(t), me_c),
                    device_id_type=MESH,
                ).start()

    for k in range(1, NP):
        d_s[0, k] = (dq_acc[k * R : (k + 1) * R, :] * scale).astype(BF)
        pltpu.make_async_remote_copy(
            src_ref=d_s.at[0, k],
            dst_ref=d_r.at[0, me_p],
            send_sem=ds_sem,
            recv_sem=dr_sem.at[0],
            device_id=(peer(k), me_c),
            device_id_type=MESH,
        ).start()

    dq, dk, dv = pair(0, R, 0)
    d_r[0, me_p] = ((dq_acc[:R] + dq) * scale).astype(BF)
    d_r[1, me_p] = ((dk_acc[0] + dk) * from_log2).astype(BF)
    d_r[2, me_p] = (dv_acc[0] + dv).astype(BF)

    def landed(j):
        part = d_r.at[j, pl.ds(0, NP - 1)]
        pltpu.make_async_copy(part, part, dr_sem.at[j]).wait()

    landed(1)
    landed(2)
    total = input_term(d_r, w1, 1) + input_term(d_r, w1, 2)
    landed(0)
    total = (total + input_term(d_r, w1, 0)).astype(BF).astype(F32)
    path = norm_grad(x[...].astype(F32), gain1[...], total).astype(BF)
    out[...] = hil[...] + path.astype(F32)

    part = qkv_s.at[:, pl.ds(0, NP - 1)]
    pltpu.make_async_copy(part, part, xs_sem).wait()
    part = mix_s.at[pl.ds(0, NP - 1)]
    pltpu.make_async_copy(part, part, ms_sem).wait()
    part = at_s.at[pl.ds(0, (inner - 1) * outer)]
    pltpu.make_async_copy(part, part, cs_sem.at[0]).wait()
    part = at_n.at[pl.ds(0, (outer - 1) * inner)]
    pltpu.make_async_copy(part, part, ns_sem).wait()
    wait_spread(a_s, cs_sem.at[1])
    wait_spread(b_s, cs_sem.at[2])
    part = g_s.at[pl.ds(0, NP - 1)]
    pltpu.make_async_copy(part, part, gs_sem).wait()
    part = d_s.at[:, pl.ds(0, NP - 1)]
    pltpu.make_async_copy(part, part, ds_sem).wait()


def shards(
    points, norm_gain_one, qkv_one, out_one, hilbert_pos,
    norm_gain_two, qkv_two, out_two, hilbert_seg, out_grad,
):
    R, D = points.shape[2], points.shape[3]
    NP, NC = lax.axis_size("patch"), lax.axis_size("curve")
    DEPTH = D // HEADS
    CAP = 2 * R // NC
    KEYS, SLOTS, chunks = NP * R, CAP * NC, D // LANES
    per = LANES // DEPTH
    sub = CAP * chunks
    vmem = pl.BlockSpec(memory_space=pltpu.VMEM)
    hbm = pl.BlockSpec(memory_space=pl.ANY)
    V = pltpu.VMEM
    DMA = pltpu.SemaphoreType.DMA
    scratch = dict(
        x=V((R, D), BF), w1=V((D, 3 * D), BF), o1=V((D, D), BF), w2=V((D, 3 * D), BF),
        o2=V((D, D), BF), og=V((R, D), BF),
        qkv_s=V((3, NP, R, LANES), BF), qkv_r=V((3, KEYS, LANES), BF),
        va=V((KEYS, 2 * LANES), BF), ex=V((per, NP, KEYS, R), BF),
        inv_all=V((KEYS, LANES), F32), mix_all=V((KEYS, LANES), F32),
        mix_s=V((NP, R, LANES), BF), mix_r=V((NP, R, LANES), BF),
        at_s=V((NC, LANES), F32), at_m=V((NC, LANES), F32),
        at_n=V((NC, LANES), F32), at_r=V((NC, LANES), F32),
        tmp=V((NC * sub, LANES), F32),
        a_s=V((NC, sub, LANES), BF), a_r=V((NC, sub, LANES), BF),
        b_s=V((NC, sub, LANES), BF), b_r=V((NC, sub, LANES), BF),
        pk=V((SLOTS, R), BF), gat=V((R, SLOTS), BF), p2=V((R, SLOTS), BF), p2t=V((SLOTS, R), BF),
        bias=V((R, R), F32), hil=V((R, D), F32),
        two=V((3, NP, R, LANES), BF), gtwo=V((NP, R, LANES), BF), dtwo=V((3, NP, R, LANES), BF),
        g_s=V((NP, R, LANES), BF), g_r=V((KEYS, LANES), BF), dq_acc=V((KEYS, LANES), F32),
        d_s=V((3, NP, R, LANES), BF), d_r=V((3, NP, R, LANES), BF),
        qm=V((per, KEYS, LANES), BF), ga=V((per, KEYS, 2 * LANES), BF),
        dk_acc=V((NP, R, LANES), F32), dv_acc=V((NP, R, LANES), F32),
        lsem=DMA((8,)), xs=DMA, xr=DMA((3,)), ms=DMA, mr=DMA, cs=DMA((3,)), cr=DMA((3,)),
        gs=DMA, gr=DMA((NP,)), ds=DMA, dr=DMA((3,)), ns=DMA, nr=DMA, xq=DMA((NP,)),
    )
    result = pl.pallas_call(
        functools.partial(kernel, NP, NC, R, D, CAP, DEPTH),
        out_shape=jax.ShapeDtypeStruct((R, D), F32),
        in_specs=[hbm] * 6 + [vmem] * 4,
        out_specs=vmem,
        scratch_shapes=list(scratch.values()),
        compiler_params=pltpu.CompilerParams(
            collective_id=0, has_side_effects=True, vmem_limit_bytes=56 * 1024 * 1024
        ),
    )(
        points.reshape(R, D), qkv_one, out_one, qkv_two, out_two, out_grad.reshape(R, D),
        norm_gain_one.reshape(1, D), norm_gain_two.reshape(1, D),
        hilbert_pos.reshape(1, R), hilbert_seg.reshape(1, R),
    )
    return result.astype(BF).reshape(points.shape)


def solution(mesh):
    in_specs = (
        P("curve", "patch", None, None), P(), P(), P(), P("curve", "patch", None),
        P(), P(), P(), P("patch", "curve", None), P("patch", "curve", None, None),
    )
    out_specs = P("curve", "patch", None, None)
    return jax.shard_map(shards, mesh=mesh, in_specs=in_specs, out_specs=out_specs, check_vma=False)
```
